768 devices in a mesh: loop: 12 (over z_hi, x), outer: 64 (over y, z_lo, core).
Axes of the slice: x: 4, y: 8, z: 12 (z_hi: 3, z_lo: 4; z = z_hi * 4 + z_lo), core: 2. Of those that a mesh axis runs over, the one named last changes fastest.
Arguments:
- note_feats: bfloat16 [196608, 1024], P(('loop', 'outer')), may hold values from -6 to 6
- ehr_feats: bfloat16 [196608, 1024], P(('loop', 'outer')), may hold values from -6 to 6
- note_head: bfloat16 [1024, 1024], replicated, may hold values from -0.1875 to 0.1875
- ehr_head: bfloat16 [1024, 1024], replicated, may hold values from -0.1875 to 0.1875
- logit_scale: float32 [1], replicated, may hold values from 8 to 24
- bias_table: float32 [16], replicated, may hold values from -3 to 0
- bias_index: int32 [196608], P(('loop', 'outer')), may hold values from 0 to 15
Outputs:
- row_loss: float32 [196608], P(('loop', 'outer'))
- note_grad: float32 [196608, 1024], P(('loop', 'outer'))
- ehr_grad: float32 [196608, 1024], P(('loop', 'outer'))
The draws below stay inside these ranges and needn't reach their ends.
All inputs are finite; a program needn't handle non-finite values.
Results may differ from the reference program's by a relative error of at most 0.0052.
Values may be sent and summed in bfloat16 or wider, within the bound.
A program may use at most 64 MiB of HBM per device.

```python
import math
import jax
import jax.numpy as jnp
from jax import lax

D = 1024
E = 1024
PAIRS_DEV = 256
SHARED = 4
BIAS_CLASSES = 16
BUNDLE = 256
WINDOW = 768
PAIRS = 196608
N_LOOP = 12
N_OUTER = 64


def with_ends(entries, rng, smallest, largest):
    spot = [jax.random.randint(jax.random.fold_in(rng, axis), (), 0, length) for axis, length in enumerate(entries.shape)]
    longest = entries.shape.index(max(entries.shape))
    beside = spot[:longest] + [(spot[longest] + 1) % entries.shape[longest]] + spot[longest + 1:]
    return entries.at[tuple(spot)].set(smallest).at[tuple(beside)].set(largest)


def block_scale(stream_key, dims, pieces, low, largest):
    factor_of = 1.0
    for position, parts in pieces:
        steps = jax.random.uniform(jax.random.fold_in(jax.random.fold_in(stream_key, 6), position), (parts,), jnp.float32, low / len(pieces), largest / len(pieces))
        factor_of = factor_of * jnp.repeat(jnp.exp(steps), dims[position] // parts).reshape((-1,) + (1,) * (len(dims) - 1 - position))
    return factor_of


def gaussian(rng, extent, width, limit, cuts=(), kind=jnp.bfloat16):
    array = width * jax.random.normal(rng, extent, jnp.float32)
    if cuts:
        array = array * block_scale(rng, extent, cuts, -0.22, 0.18)
    return jnp.clip(array, -limit, limit).astype(kind)


def setup_inputs(seed: int = 0) -> dict:
    key_list = jax.random.split(jax.random.key(seed), 8)
    return {
        "note_feats": gaussian(key_list[0], (PAIRS, D), 1.0, 6.0, ((0, 768),)),
        "ehr_feats": gaussian(key_list[1], (PAIRS, D), 1.0, 6.0, ((0, 768),)),
        "note_head": gaussian(key_list[2], (D, E), D ** -0.5, 0.1875),
        "ehr_head": gaussian(key_list[3], (D, E), D ** -0.5, 0.1875),
        "logit_scale": jnp.clip(jnp.exp(jax.random.uniform(key_list[4], (1,), jnp.float32, math.log(8.0), math.log(24.0))), 8.0, 24.0),
        "bias_table": jnp.clip(jax.random.uniform(key_list[5], (BIAS_CLASSES,), jnp.float32, -3.0, 0.0), -3.0, 0.0),
        "bias_index": with_ends(jax.random.randint(key_list[6], (PAIRS,), 0, BIAS_CLASSES), jax.random.fold_in(key_list[6], 1), 0, BIAS_CLASSES - 1).astype(jnp.int32),
    }


def unit_rows(features, head_matrix):
    projected = jnp.dot(features, head_matrix, preferred_element_type=jnp.float32)
    inverse = lax.rsqrt(lax.optimization_barrier(jnp.sum(projected * projected, axis=-1, keepdims=True)) + 1e-06)
    return (projected * inverse, inverse)

def unit_back(normed, inverse, upstream, head_matrix):
    radial = lax.optimization_barrier(jnp.sum(normed * upstream, axis=-1, keepdims=True))
    pre_grad = (inverse * (upstream - normed * radial)).astype(jnp.bfloat16)
    return jnp.dot(pre_grad, head_matrix.T, preferred_element_type=jnp.float32)

def reference(note_feats, ehr_feats, note_head, ehr_head, logit_scale, bias_table, bias_index):
    note_unit, note_inverse = unit_rows(note_feats, note_head)
    ehr_unit, ehr_inverse = unit_rows(ehr_feats, ehr_head)
    notes = note_unit.astype(jnp.bfloat16).reshape(N_LOOP, N_OUTER, PAIRS_DEV, E)
    records = ehr_unit.astype(jnp.bfloat16).reshape(N_LOOP, N_OUTER, PAIRS_DEV, E)
    shared = notes[:, :, :SHARED].reshape(N_LOOP, BUNDLE, E).astype(jnp.float32)
    below = jnp.roll(shared, 1, 0)
    above = jnp.roll(shared, -1, 0)
    multiplier = logit_scale[0]
    offsets = bias_table[bias_index].reshape(N_LOOP, N_OUTER, PAIRS_DEV, 1)
    rec32 = records.astype(jnp.float32)
    notes32 = notes.astype(jnp.float32)
    local_sim = jnp.einsum('lope,loqe->lopq', rec32, notes32)
    below_sim = jnp.einsum('lope,lbe->lopb', rec32, below)
    above_sim = jnp.einsum('lope,lbe->lopb', rec32, above)
    logits = multiplier * jnp.concatenate([local_sim, below_sim, above_sim], axis=-1) + offsets
    columns = lax.broadcasted_iota(jnp.int32, (PAIRS_DEV, WINDOW), 1)
    row_ids = lax.broadcasted_iota(jnp.int32, (PAIRS_DEV, WINDOW), 0)
    labels = jnp.where(columns == row_ids, 1.0, -1.0).astype(jnp.float32)
    margins = -labels * logits
    row_loss = lax.optimization_barrier(jnp.mean(jax.nn.softplus(margins), axis=-1)).reshape(PAIRS)
    slopes = (-labels * jax.nn.sigmoid(margins)).astype(jnp.bfloat16).astype(jnp.float32)
    slope_local = slopes[..., :PAIRS_DEV]
    slope_below = slopes[..., PAIRS_DEV:PAIRS_DEV + BUNDLE]
    slope_above = slopes[..., PAIRS_DEV + BUNDLE:]
    record_upstream = multiplier * (jnp.einsum('lopq,loqe->lope', slope_local, notes32) + jnp.einsum('lopb,lbe->lope', slope_below, below) + jnp.einsum('lopb,lbe->lope', slope_above, above))
    local_grad = multiplier * jnp.einsum('lopq,lope->loqe', slope_local, rec32)
    below_grad = multiplier * jnp.einsum('lopb,lope->lbe', slope_below, rec32)
    above_grad = multiplier * jnp.einsum('lopb,lope->lbe', slope_above, rec32)
    shared_up = (jnp.roll(below_grad, -1, 0) + jnp.roll(above_grad, 1, 0)).reshape(N_LOOP, N_OUTER, SHARED, E)
    note_upstream = jnp.concatenate([local_grad[:, :, :SHARED] + shared_up, local_grad[:, :, SHARED:]], axis=2)
    note_grad = unit_back(note_unit, note_inverse, note_upstream.reshape(PAIRS, E), note_head)
    ehr_grad = unit_back(ehr_unit, ehr_inverse, record_upstream.reshape(PAIRS, E), ehr_head)
    return (row_loss, note_grad, ehr_grad)
```

```python
import functools

import jax
import jax.numpy as jnp
from jax import lax
from jax.experimental import pallas as pl
from jax.experimental.pallas import tpu as pltpu
from jax.sharding import PartitionSpec as P

SHARED = 4
Z = 4
CORES = 2
BLOCK = SHARED * Z
MESH = pl.DeviceIdType.MESH
NT = (((1,), (1,)), ((), ()))
TN = (((0,), (0,)), ((), ()))


def dot(a, b, dims=(((1,), (0,)), ((), ()))):
    return lax.dot_general(a, b, dims, preferred_element_type=jnp.float32)


def terms(margins):
    t = jnp.exp(-jnp.abs(margins))
    r = 1.0 / (1.0 + t)
    return jnp.maximum(margins, 0.0) + jnp.log1p(t), jnp.where(margins >= 0.0, r, t * r)


def upper_half(shape):
    return lax.broadcasted_iota(jnp.int32, shape, 0) < SHARED


def pack(rows):
    w = rows.shape[1] // 4
    c = [rows[:, q * w : (q + 1) * w] for q in range(4)]
    up = upper_half(c[0].shape)
    lo = jnp.where(up, c[0], pltpu.roll(c[1], SHARED, 0))
    hi = jnp.where(up, c[2], pltpu.roll(c[3], SHARED, 0))
    return jnp.concatenate([lo, hi], axis=0)


def unpack_pair(first, second):
    up = upper_half((8, first.shape[1]))
    out = []
    for half in range(2):
        a, b = first[half * 8 : half * 8 + 8], second[half * 8 : half * 8 + 8]
        out.append(jnp.where(up, a, pltpu.roll(b, SHARED, 0)))
        out.append(jnp.where(up, pltpu.roll(a, SHARED, 0), b))
    return jnp.concatenate(out, axis=1)


def kernel(
    n_loop, ring,
    nf_hbm, ef_hbm, nh_hbm, eh_hbm, scale_ref, table_ref, index_ref,
    loss_ref, ng_hbm, eg_hbm,
    nf, ef, nh, eh, nu, ru, ninv, rinv, ne, re, off, off_out,
    pieces, own_piece, W, G, S, R, back_out, back, slopes, local_slopes,
    lossacc, loss_out, loss_in, rup, rup_out, rup_in, nup, pre, out_n, out_e, tail,
    load_sem, store_sem, piece_send, piece_recv, ag_send, ag_recv, rs_send, rs_recv,
    back_send, back_recv, sib_send, sib_recv,
):
    pairs, width = nf.shape
    far = ring // 2
    tile = min(256, width)
    tiles = width // tile
    l, o = lax.axis_index("loop"), lax.axis_index("outer")
    c, z, y = lax.rem(o, CORES), lax.rem(o // CORES, Z), o // (CORES * Z)

    def outer(yy, zz, cc):
        return (yy * Z + zz) * CORES + cc

    below, above = lax.rem(l + n_loop - 1, n_loop), lax.rem(l + 1, n_loop)
    ahead = (l, outer(lax.rem(y + 1, ring), z, c))
    behind = (l, outer(lax.rem(y + ring - 1, ring), z, c))
    sibling = (l, outer(y, z, 1 - c))
    zs = [lax.rem(z + d, Z) for d in range(Z)]

    barrier = pltpu.get_barrier_semaphore()
    partners = [ahead, behind, sibling]
    partners += [(p, outer(y, zz, c)) for p in (below, above) for zz in zs]
    for partner in partners:
        pl.semaphore_signal(barrier, inc=1, device_id=partner, device_id_type=MESH)

    loads = [
        pltpu.make_async_copy(src, dst, load_sem.at[i])
        for i, (src, dst) in enumerate(((nh_hbm, nh), (nf_hbm, nf), (eh_hbm, eh), (ef_hbm, ef)))
    ]
    for load in loads:
        load.start()

    def remote(src, dst, send, recv, device):
        return pltpu.make_async_remote_copy(
            src_ref=src, dst_ref=dst, send_sem=send, recv_sem=recv, device_id=device, device_id_type=MESH
        )

    def project(feats, head, unit):
        def step(j, carry):
            cols = pl.ds(pl.multiple_of(j * tile, tile), tile)
            unit[:, cols] = dot(feats[...], head[:, cols])
            return carry

        lax.fori_loop(0, tiles, step, 0)

    def normalise(unit, inverse, emb):
        step_rows = min(64, pairs)

        def step(j, carry):
            rows = pl.ds(pl.multiple_of(j * step_rows, step_rows), step_rows)
            p = unit[rows, :]
            inv = lax.rsqrt(jnp.sum(p * p, axis=-1, keepdims=True) + 1e-06)
            u = p * inv
            inverse[rows, :] = inv
            unit[rows, :] = u
            emb[rows, :] = u.astype(jnp.bfloat16)
            return carry

        lax.fori_loop(0, pairs // step_rows, step, 0)

    loads[0].wait()
    loads[1].wait()
    project(nf, nh, nu)
    top = nu[0:8, :]
    top = top * lax.rsqrt(jnp.sum(top * top, axis=-1, keepdims=True) + 1e-06)
    own_piece[...] = pack(top).astype(jnp.bfloat16)
    pl.semaphore_wait(barrier, len(partners))
    piece_copies = []
    for side, pod in ((0, above), (1, below)):
        for d in range(Z):
            k = side * Z + d
            piece_copies.append(
                remote(own_piece, pieces.at[k], piece_send.at[k], piece_recv.at[k], (pod, outer(y, zs[d], c)))
            )
            piece_copies[-1].start()
    normalise(nu, ninv, ne)

    loads[2].wait()
    loads[3].wait()
    project(ef, eh, ru)
    normalise(ru, rinv, re.at[pl.ds(0, pairs)])
    index = index_ref[...]
    offsets = jnp.zeros(index.shape, jnp.float32)
    for k in range(table_ref.shape[0]):
        offsets = jnp.where(index == k, table_ref[k], offsets)
    off_out[...] = jnp.broadcast_to(offsets, off_out.shape)
    sib_rec = remote(re.at[pl.ds(0, pairs)], re.at[pl.ds(pairs, pairs)], sib_send.at[0], sib_recv.at[0], sibling)
    sib_off = remote(off_out, off, sib_send.at[1], sib_recv.at[1], sibling)
    sib_rec.start()
    sib_off.start()

    def reach(side, way):
        return far if (side == 0) == (way == 1) else far - 1

    def slot(side, way, dist):
        if dist == 0:
            return side
        if dist == far:
            return 2 + 4 * (far - 1) + side
        return 2 + 4 * (dist - 1) + 2 * (way < 0) + side

    def rows_of(s):
        return pl.ds(s * BLOCK, BLOCK)

    scale = scale_ref[0]
    for copy in piece_copies:
        copy.wait_recv()
    for side in range(2):
        p = [pieces[side * Z + d].astype(jnp.float32) for d in range(Z)]
        block = jnp.concatenate([unpack_pair(p[0], p[1]), unpack_pair(p[2], p[3])], axis=0)
        W[side * BLOCK : (side + 1) * BLOCK, :] = block.astype(jnp.bfloat16)

    gathers = {}

    def forward(side, way, dist):
        src, dst = slot(side, way, dist), slot(side, way, dist + 1)
        copy = remote(
            W.at[rows_of(src)], W.at[rows_of(dst)], ag_send.at[dst - 2], ag_recv.at[dst - 2],
            ahead if way == 1 else behind,
        )
        copy.start()
        gathers[side, way, dist + 1] = copy

    chains = [(0, 1), (1, -1), (1, 1), (0, -1)]
    for side, way in chains:
        forward(side, way, 0)

    sims = dot(ne[...], re[0:pairs, :], NT)
    logits = scale * sims + offsets
    positive = lax.broadcasted_iota(jnp.int32, logits.shape, 0) == lax.broadcasted_iota(jnp.int32, logits.shape, 1)
    softplus, sigmoid = terms(jnp.where(positive, -logits, logits))
    local_slopes[...] = jnp.where(positive, -sigmoid, sigmoid).astype(jnp.bfloat16)
    lossacc[:, 0:pairs] = jnp.sum(softplus.reshape(pairs // 8, 8, pairs), axis=0)
    lossacc[:, pairs:] = jnp.zeros((8, pairs), jnp.float32)

    sib_off.wait_recv()
    sib_rec.wait_recv()
    all_offsets = jnp.concatenate([off_out[0:1, :], off[0:1, :]], axis=1)

    def notes(first, count):
        rows = slice(first * BLOCK, (first + count) * BLOCK)
        n = count * BLOCK
        logits = scale * dot(W[rows, :], re[...], NT) + all_offsets
        softplus, sigmoid = terms(logits)
        lossacc[...] += jnp.sum(softplus.reshape(n // 8, 8, 2 * pairs), axis=0)
        s = sigmoid.astype(jnp.bfloat16)
        slopes[rows, :] = s
        G[rows, :] = dot(s, re[...])

    reduces = {}

    def reduce_from(side, way, dist):
        s = slot(side, way, dist)
        rows = slice(s * BLOCK, (s + 1) * BLOCK)
        total = G[rows, :]
        if dist < reach(side, way):
            reduces[side, way, dist + 1].wait_recv()
            total = total + R[slot(side, way, dist + 1) - 2].astype(jnp.float32)
        S[s - 2] = total.astype(jnp.bfloat16)
        copy = remote(
            S.at[s - 2], R.at[s - 2], rs_send.at[s - 2], rs_recv.at[s - 2], behind if way == 1 else ahead
        )
        copy.start()
        reduces[side, way, dist] = copy

    notes(0, 2)
    for dist in range(1, far):
        for side, way in chains:
            gathers[side, way, dist].wait_recv()
            if dist < reach(side, way):
                forward(side, way, dist)
        notes(2 + 4 * (dist - 1), 4)
    short = [(1, 1), (0, -1)]
    long = [(0, 1), (1, -1)]
    if far > 1:
        for side, way in short:
            reduce_from(side, way, far - 1)
    for side, way in long:
        gathers[side, way, far].wait_recv()
    notes(2 + 4 * (far - 1), 2)
    for side, way in long:
        reduce_from(side, way, far)

    def upstream_sibling(j, carry):
        cols = pl.ds(pl.multiple_of(j * tile, tile), tile)
        rup_out[:, cols] = dot(slopes[:, pairs:], W[:, cols], TN)
        return carry

    def upstream_own(j, carry):
        cols = pl.ds(pl.multiple_of(j * tile, tile), tile)
        rup[:, cols] = dot(slopes[:, 0:pairs], W[:, cols], TN) + dot(local_slopes[...], ne[:, cols], TN)
        return carry

    def upstream_notes(j, carry):
        cols = pl.ds(pl.multiple_of(j * tile, tile), tile)
        nup[:, cols] = scale * dot(local_slopes[...], re[0:pairs, cols])
        return carry

    def back_grad(head, out):
        def step(j, carry):
            cols = pl.ds(pl.multiple_of(j * tile, tile), tile)
            out[:, cols] = dot(pre[...], head[cols, :], NT)
            return carry

        lax.fori_loop(0, tiles, step, 0)

    def pre_grads(unit, inverse, upstream):
        step_rows = min(64, pairs)

        def step(j, carry):
            rows = pl.ds(pl.multiple_of(j * step_rows, step_rows), step_rows)
            u, up = unit[rows, :], upstream(rows)
            radial = jnp.sum(u * up, axis=-1, keepdims=True)
            pre[rows, :] = (inverse[rows, :] * (up - u * radial)).astype(jnp.bfloat16)
            return carry

        lax.fori_loop(0, pairs // step_rows, step, 0)

    def reduce_step(dist):
        if 1 <= dist - 1:
            for side, way in short:
                reduce_from(side, way, dist - 1)
        if 1 <= dist:
            for side, way in long:
                reduce_from(side, way, dist)

    lax.fori_loop(0, tiles, upstream_sibling, 0)
    loss_out[...] = lossacc[:, pairs:]
    sib_rup = remote(rup_out, rup_in, sib_send.at[2], sib_recv.at[2], sibling)
    sib_loss = remote(loss_out, loss_in, sib_send.at[3], sib_recv.at[3], sibling)
    sib_rup.start()
    sib_loss.start()
    stores = []

    def filler_a():
        lax.fori_loop(0, tiles, upstream_own, 0)

    def filler_b():
        lax.fori_loop(0, tiles, upstream_notes, 0)
        pre_grads(nu, ninv, lambda rows: nup[rows, :])
        back_grad(nh, out_n)
        copy = pltpu.make_async_copy(
            out_n.at[pl.ds(8, pairs - 8)], ng_hbm.at[pl.ds(8, pairs - 8)], store_sem.at[0]
        )
        copy.start()
        stores.append(copy)

    def filler_c():
        sib_rup.wait_recv()
        sib_loss.wait_recv()
        loss = jnp.sum(lossacc[:, 0:pairs] + loss_in[...], axis=0, keepdims=True)
        loss_ref[...] = loss * (1.0 / (pairs + ring * Z * CORES * SHARED * 2))
        pre_grads(ru, rinv, lambda rows: scale * (rup[rows, :] + rup_in[rows, :]))
        back_grad(eh, out_e)
        copy = pltpu.make_async_copy(out_e, eg_hbm, store_sem.at[1])
        copy.start()
        stores.append(copy)

    fillers = [filler_a, filler_b, filler_c]
    for dist in range(far - 1, 0, -1):
        reduce_step(dist)
        if fillers:
            fillers.pop(0)()
    for filler in fillers:
        filler()

    returns = []
    for side in range(2):
        total = G[side * BLOCK : (side + 1) * BLOCK, :]
        for way in (1, -1):
            if reach(side, way) > 0:
                reduces[side, way, 1].wait_recv()
                total = total + R[slot(side, way, 1) - 2].astype(jnp.float32)
        total = scale * total
        for d in range(Z):
            half = total[(d // 2) * 8 : (d // 2) * 8 + 8, :]
            if d % 2:
                half = pltpu.roll(half, SHARED, 0)
            k = side * Z + d
            back_out[k] = pack(half).astype(jnp.bfloat16)
            owner_z = lax.rem(z + Z - d, Z)
            copy = remote(
                back_out.at[k], back.at[k], back_send.at[k], back_recv.at[k],
                (below if side == 0 else above, outer(y, owner_z, c)),
            )
            copy.start()
            returns.append(copy)

    total = None
    for k, copy in enumerate(returns):
        copy.wait_recv()
        part = back[k].astype(jnp.float32)
        total = part if total is None else total + part
    lo, hi = total[0:8], total[8:16]
    spread = jnp.concatenate([lo, pltpu.roll(lo, SHARED, 0), hi, pltpu.roll(hi, SHARED, 0)], axis=1)
    up = nup[0:8, :] + jnp.where(upper_half(spread.shape), spread, 0.0)
    u = nu[0:8, :]
    radial = jnp.sum(u * up, axis=-1, keepdims=True)
    g = (ninv[0:8, :] * (up - u * radial)).astype(jnp.bfloat16)
    tail[...] = dot(g, nh[...], NT)
    last = pltpu.make_async_copy(tail, ng_hbm.at[pl.ds(0, 8)], store_sem.at[2])
    last.start()
    stores.append(last)

    sent = piece_copies + list(gathers.values()) + list(reduces.values()) + returns
    for copy in sent + [sib_rec, sib_off, sib_rup, sib_loss]:
        copy.wait_send()
    for copy in stores:
        copy.wait()


def per_device(n_loop, n_outer, note_feats, ehr_feats, note_head, ehr_head, logit_scale, bias_table, bias_index):
    pairs, width = note_feats.shape
    emb = note_head.shape[1]
    ring = n_outer // (Z * CORES)
    blocks = 2 * ring
    held = blocks * BLOCK
    bf16, f32 = jnp.bfloat16, jnp.float32
    vmem = pltpu.VMEM
    dma = pltpu.SemaphoreType.DMA
    hbm = pl.BlockSpec(memory_space=pl.ANY)
    smem = pl.BlockSpec(memory_space=pltpu.SMEM)
    whole = pl.BlockSpec(memory_space=pltpu.VMEM)
    loss, note_grad, ehr_grad = pl.pallas_call(
        functools.partial(kernel, n_loop, ring),
        out_shape=(
            jax.ShapeDtypeStruct((1, pairs), f32),
            jax.ShapeDtypeStruct((pairs, width), f32),
            jax.ShapeDtypeStruct((pairs, width), f32),
        ),
        in_specs=[hbm] * 4 + [smem, smem, whole],
        out_specs=(whole, hbm, hbm),
        scratch_shapes=[
            vmem((pairs, width), bf16),
            vmem((pairs, width), bf16),
            vmem((width, emb), bf16),
            vmem((width, emb), bf16),
            vmem((pairs, emb), f32),
            vmem((pairs, emb), f32),
            vmem((pairs, 1), f32),
            vmem((pairs, 1), f32),
            vmem((pairs, emb), bf16),
            vmem((2 * pairs, emb), bf16),
            vmem((8, pairs), f32),
            vmem((8, pairs), f32),
            vmem((2 * Z, BLOCK, emb // 4), bf16),
            vmem((BLOCK, emb // 4), bf16),
            vmem((held, emb), bf16),
            vmem((held, emb), f32),
            vmem((blocks - 2, BLOCK, emb), bf16),
            vmem((blocks - 2, BLOCK, emb), bf16),
            vmem((2 * Z, BLOCK, emb // 4), bf16),
            vmem((2 * Z, BLOCK, emb // 4), bf16),
            vmem((held, 2 * pairs), bf16),
            vmem((pairs, pairs), bf16),
            vmem((8, 2 * pairs), f32),
            vmem((8, pairs), f32),
            vmem((8, pairs), f32),
            vmem((pairs, emb), f32),
            vmem((pairs, emb), f32),
            vmem((pairs, emb), f32),
            vmem((pairs, emb), f32),
            vmem((pairs, emb), bf16),
            vmem((pairs, width), f32),
            vmem((pairs, width), f32),
            vmem((8, width), f32),
            dma((4,)),
            dma((3,)),
            dma((2 * Z,)),
            dma((2 * Z,)),
            dma((blocks - 2,)),
            dma((blocks - 2,)),
            dma((blocks - 2,)),
            dma((blocks - 2,)),
            dma((2 * Z,)),
            dma((2 * Z,)),
            dma((4,)),
            dma((4,)),
        ],
        compiler_params=pltpu.CompilerParams(
            collective_id=0, has_side_effects=True, vmem_limit_bytes=48 * 1024 * 1024
        ),
    )(note_feats, ehr_feats, note_head, ehr_head, logit_scale, bias_table, bias_index.reshape(1, pairs))
    return loss.reshape(pairs), note_grad, ehr_grad


def solution(mesh):
    return jax.shard_map(
        functools.partial(per_device, mesh.shape["loop"], mesh.shape["outer"]),
        mesh=mesh,
        in_specs=(
            P(("loop", "outer"), None),
            P(("loop", "outer"), None),
            P(),
            P(),
            P(),
            P(),
            P(("loop", "outer")),
        ),
        out_specs=(P(("loop", "outer")), P(("loop", "outer"), None), P(("loop", "outer"), None)),
        check_vma=False,
    )
```

```python
import functools

import jax
import jax.numpy as jnp
from jax import lax
from jax.experimental import pallas as pl
from jax.experimental.pallas import tpu as pltpu
from jax.sharding import PartitionSpec as P

SHARED = 4
Z = 4
CORES = 2
X = 4
BLOCK = SHARED * Z
MESH = pl.DeviceIdType.MESH
NT = (((1,), (1,)), ((), ()))
TN = (((0,), (0,)), ((), ()))


def dot(a, b, dims=(((1,), (0,)), ((), ()))):
    return lax.dot_general(a, b, dims, preferred_element_type=jnp.float32)


def terms(margins):
    t = jnp.exp(-jnp.abs(margins))
    r = 1.0 / (1.0 + t)
    return jnp.maximum(margins, 0.0) + jnp.log1p(t), jnp.where(margins >= 0.0, r, t * r)


def upper_half(shape):
    return lax.broadcasted_iota(jnp.int32, shape, 0) < SHARED


def pack(rows):
    w = rows.shape[1] // 4
    c = [rows[:, q * w : (q + 1) * w] for q in range(4)]
    up = upper_half(c[0].shape)
    lo = jnp.where(up, c[0], pltpu.roll(c[1], SHARED, 0))
    hi = jnp.where(up, c[2], pltpu.roll(c[3], SHARED, 0))
    return jnp.concatenate([lo, hi], axis=0)


def unpack_pair(first, second):
    up = upper_half((8, first.shape[1]))
    out = []
    for half in range(2):
        a, b = first[half * 8 : half * 8 + 8], second[half * 8 : half * 8 + 8]
        out.append(jnp.where(up, a, pltpu.roll(b, SHARED, 0)))
        out.append(jnp.where(up, pltpu.roll(a, SHARED, 0), b))
    return jnp.concatenate(out, axis=1)


def kernel(
    n_loop, ring,
    nf_hbm, ef_hbm, nh_hbm, eh_hbm, scale_hbm, table_hbm, index_hbm,
    loss_hbm, ng_hbm, eg_hbm,
    nf, ef, nh, eh, scale_ref, table_ref, index_ref, nu, ru, ninv, rinv, ne, re, off, off_out,
    pieces_a, pieces_b, own_piece, W, G, S, R, back_out, back, back_sum, slopes, local_slopes,
    lossacc, loss_out, loss_in, rup, rup_out, rup_in, nup, pre, ng, eg, loss_ref,
    load_sem, store_sem, piece_send, recv_a, recv_b, ag_send, ag_recv, rs_send, rs_recv,
    back_send, back_recv, sib_send, sib_recv,
):
    pairs, width = nf.shape
    tile = min(256, width)
    tiles = width // tile
    l, o = lax.axis_index("loop"), lax.axis_index("outer")
    c, z, y = lax.rem(o, CORES), lax.rem(o // CORES, Z), o // (CORES * Z)
    x = lax.rem(l, X)
    z_first = lax.rem((x + 1) // 2, 2) == 0
    side_a = x // 2
    side_b = 1 - side_a
    pod_a = lax.rem(l + n_loop - 1 + 2 * side_a, n_loop)
    pod_b = lax.rem(l + n_loop + 1 - 2 * side_a, n_loop)

    def outer(yy, zz, cc):
        return (yy * Z + zz) * CORES + cc

    below, above = lax.rem(l + n_loop - 1, n_loop), lax.rem(l + 1, n_loop)
    ys = [lax.rem(y + d, ring) for d in range(ring)]
    zs = [lax.rem(z + d, Z) for d in range(Z)]
    ys_back = [lax.rem(y + ring - d, ring) for d in range(ring)]
    zs_back = [lax.rem(z + Z - d, Z) for d in range(Z)]
    sibling = (l, outer(y, z, 1 - c))

    barrier = pltpu.get_barrier_semaphore()
    partners = [sibling]
    partners += [(l, outer(yy, z, c)) for yy in ys[1:]] + [(l, outer(y, zz, c)) for zz in zs[1:]]
    for pod in (below, above):
        partners += [(pod, outer(yy, z, c)) for yy in ys] + [(pod, outer(y, zz, c)) for zz in zs[1:]]
    for partner in partners:
        pl.semaphore_signal(barrier, inc=1, device_id=partner, device_id_type=MESH)

    loads = [
        pltpu.make_async_copy(src, dst, load_sem.at[i])
        for i, (src, dst) in enumerate((
            (nh_hbm, nh), (nf_hbm, nf), (eh_hbm, eh), (ef_hbm, ef),
            (scale_hbm, scale_ref), (table_hbm, table_ref), (index_hbm, index_ref),
        ))
    ]
    for load in loads:
        load.start()

    def remote(src, dst, send, recv, device):
        return pltpu.make_async_remote_copy(
            src_ref=src, dst_ref=dst, send_sem=send, recv_sem=recv, device_id=device, device_id_type=MESH
        )

    def project(feats, head, unit):
        def step(j, carry):
            cols = pl.ds(pl.multiple_of(j * tile, tile), tile)
            unit[:, cols] = dot(feats[...], head[:, cols])
            return carry

        lax.fori_loop(0, tiles, step, 0)

    def normalise(unit, inverse, emb):
        step_rows = min(64, pairs)

        def step(j, carry):
            rows = pl.ds(pl.multiple_of(j * step_rows, step_rows), step_rows)
            p = unit[rows, :]
            inv = lax.rsqrt(jnp.sum(p * p, axis=-1, keepdims=True) + 1e-06)
            u = p * inv
            inverse[rows, :] = inv
            unit[rows, :] = u
            emb[rows, :] = u.astype(jnp.bfloat16)
            return carry

        lax.fori_loop(0, pairs // step_rows, step, 0)

    loads[0].wait()
    loads[1].wait()
    project(nf, nh, nu)
    top = nu[0:8, :]
    top = top * lax.rsqrt(jnp.sum(top * top, axis=-1, keepdims=True) + 1e-06)
    own_piece[...] = pack(top).astype(jnp.bfloat16)
    pl.semaphore_wait(barrier, len(partners))

    def piece_sends(along_z):
        copies = []
        for side, pod in enumerate((above, below)):
            for d in range(Z if along_z else ring):
                device = (pod, outer(y, zs[d], c) if along_z else outer(ys[d], z, c))
                landing, recv = (pieces_a, recv_a) if along_z else (pieces_b, recv_b)
                copies.append(
                    remote(own_piece, landing.at[d], piece_send.at[side * ring + d], recv.at[d], device)
                )
        return copies

    @pl.when(z_first)
    def _():
        for copy in piece_sends(True):
            copy.start()

    @pl.when(jnp.logical_not(z_first))
    def _():
        for copy in piece_sends(False):
            copy.start()

    normalise(nu, ninv, ne)

    for load in loads[2:]:
        load.wait()
    project(ef, eh, ru)
    normalise(ru, rinv, re.at[pl.ds(0, pairs)])
    index = index_ref[...]
    offsets = jnp.zeros(index.shape, jnp.float32)
    for k in range(table_ref.shape[0]):
        offsets = jnp.where(index == k, table_ref[k], offsets)
    off_out[...] = jnp.broadcast_to(offsets, off_out.shape)
    sib_rec = remote(re.at[pl.ds(0, pairs)], re.at[pl.ds(pairs, pairs)], sib_send.at[0], sib_recv.at[0], sibling)
    sib_off = remote(off_out, off, sib_send.at[1], sib_recv.at[1], sibling)
    sib_rec.start()
    sib_off.start()
    scale = scale_ref[0]

    rows_a, rows_b = BLOCK, SHARED * ring
    groups = [[("a", 0), ("b", 0)], [], [], []]
    for dist in range(1, ring // 2 + 1):
        groups[min(dist, 3)] += [("a", d) for d in sorted({dist, ring - dist})]
    for group, d in ((1, 1), (2, 3), (3, 2)):
        groups[group].append(("b", d))
    place, spans, first = {}, [], 0
    for group in groups:
        start = first
        for kind, d in group:
            size = rows_a if kind == "a" else rows_b
            place[kind, d] = (first, size)
            first += size
        spans.append((start, first))
    sem_of = {key: i for i, key in enumerate(k for k in place if k[1])}

    def gather(kind, d):
        (src, size), (dst, _) = place[kind, 0], place[kind, d]
        i = sem_of[kind, d]
        device = (l, outer(ys[d], z, c)) if kind == "a" else (l, outer(y, zs[d], c))
        return remote(W.at[pl.ds(src, size)], W.at[pl.ds(dst, size)], ag_send.at[i], ag_recv.at[i], device)

    def give_back(kind, d):
        rows = pl.ds(*place[kind, d])
        i = sem_of[kind, d]
        device = (l, outer(ys_back[d], z, c)) if kind == "a" else (l, outer(y, zs_back[d], c))
        return remote(S.at[rows], R.at[rows], rs_send.at[i], rs_recv.at[i], device)

    gathers = {key: gather(*key) for key in sem_of}
    reduces = {key: give_back(*key) for key in sem_of}

    def collect(kind, landing, recv, count):
        for d in range(count):
            remote(own_piece, landing.at[d], piece_send.at[0], recv.at[d], sibling).wait_recv()
        p = [landing[d].astype(jnp.float32) for d in range(count)]
        block = jnp.concatenate([unpack_pair(p[d], p[d + 1]) for d in range(0, count, 2)], axis=0)
        start, size = place[kind, 0]
        W[start : start + size, :] = block.astype(jnp.bfloat16)
        for key in sem_of:
            if key[0] == kind:
                gathers[key].start()

    sims = dot(ne[...], re[0:pairs, :], NT)
    logits = scale * sims + offsets
    positive = lax.broadcasted_iota(jnp.int32, logits.shape, 0) == lax.broadcasted_iota(jnp.int32, logits.shape, 1)
    softplus, sigmoid = terms(jnp.where(positive, -logits, logits))
    local_slopes[...] = jnp.where(positive, -sigmoid, sigmoid).astype(jnp.bfloat16)
    lossacc[:, 0:pairs] = jnp.sum(softplus.reshape(pairs // 8, 8, pairs), axis=0)
    lossacc[:, pairs:] = jnp.zeros((8, pairs), jnp.float32)

    collect("b", pieces_b, recv_b, ring)
    collect("a", pieces_a, recv_a, Z)

    def back_grad(head, out):
        def step(j, carry):
            cols = pl.ds(pl.multiple_of(j * tile, tile), tile)
            out[:, cols] = dot(pre[...], head[cols, :], NT)
            return carry

        lax.fori_loop(0, tiles, step, 0)

    def pre_grads(unit, inverse, upstream):
        step_rows = min(64, pairs)

        def step(j, carry):
            rows = pl.ds(pl.multiple_of(j * step_rows, step_rows), step_rows)
            u, up = unit[rows, :], upstream(rows)
            radial = jnp.sum(u * up, axis=-1, keepdims=True)
            pre[rows, :] = (inverse[rows, :] * (up - u * radial)).astype(jnp.bfloat16)
            return carry

        lax.fori_loop(0, pairs // step_rows, step, 0)

    sib_off.wait_recv()
    sib_rec.wait_recv()
    all_offsets = jnp.concatenate([off_out[0:1, :], off[0:1, :]], axis=1)

    def work(g):
        for key in groups[g]:
            if key[1]:
                gathers[key].wait_recv()
        start, stop = spans[g]
        n = stop - start
        if n == 0:
            return
        logits = scale * dot(W[start:stop, :], re[...], NT) + all_offsets
        softplus, sigmoid = terms(logits)
        lossacc[...] += jnp.sum(softplus.reshape(n // 8, 8, 2 * pairs), axis=0)
        s = sigmoid.astype(jnp.bfloat16)
        slopes[start:stop, :] = s
        grads = dot(s, re[...])
        if g == 0:
            G[...] = grads
        else:
            S[start:stop, :] = grads.astype(jnp.bfloat16)
            for key in groups[g]:
                reduces[key].start()

    work(0)

    def upstream_notes(j, carry):
        cols = pl.ds(pl.multiple_of(j * tile, tile), tile)
        nup[:, cols] = scale * dot(local_slopes[...], re[0:pairs, cols])
        return carry

    lax.fori_loop(0, tiles, upstream_notes, 0)
    pre_grads(nu, ninv, lambda rows: nup[rows, :])
    back_grad(nh, ng)
    stores = [
        pltpu.make_async_copy(ng.at[pl.ds(8, pairs - 8)], ng_hbm.at[pl.ds(8, pairs - 8)], store_sem.at[0]),
        pltpu.make_async_copy(eg, eg_hbm, store_sem.at[1]),
        pltpu.make_async_copy(loss_ref, loss_hbm, store_sem.at[2]),
        pltpu.make_async_copy(ng.at[pl.ds(0, 8)], ng_hbm.at[pl.ds(0, 8)], store_sem.at[3]),
    ]
    stores[0].start()
    for g in (1, 2, 3):
        work(g)

    def upstream_sibling(j, carry):
        cols = pl.ds(pl.multiple_of(j * tile, tile), tile)
        rup_out[:, cols] = dot(slopes[:, pairs:], W[:, cols], TN)
        return carry

    def upstream_own(j, carry):
        cols = pl.ds(pl.multiple_of(j * tile, tile), tile)
        rup[:, cols] = dot(slopes[:, 0:pairs], W[:, cols], TN) + dot(local_slopes[...], ne[:, cols], TN)
        return carry

    lax.fori_loop(0, tiles, upstream_sibling, 0)
    loss_out[...] = lossacc[:, pairs:]
    sib_rup = remote(rup_out, rup_in, sib_send.at[2], sib_recv.at[2], sibling)
    sib_loss = remote(loss_out, loss_in, sib_send.at[3], sib_recv.at[3], sibling)
    sib_rup.start()
    sib_loss.start()
    lax.fori_loop(0, tiles, upstream_own, 0)
    sib_rup.wait_recv()
    sib_loss.wait_recv()
    loss = jnp.sum(lossacc[:, 0:pairs] + loss_in[...], axis=0, keepdims=True)
    loss_ref[...] = loss * (1.0 / (pairs + ring * Z * CORES * SHARED * 2))
    pre_grads(ru, rinv, lambda rows: scale * (rup[rows, :] + rup_in[rows, :]))
    back_grad(eh, eg)
    stores[1].start()
    stores[2].start()

    returns = []
    for kind, pod, side, count in (("b", pod_b, side_b, ring), ("a", pod_a, side_a, Z)):
        start, size = place[kind, 0]
        total = G[start : start + size, :]
        for key in sem_of:
            if key[0] == kind:
                reduces[key].wait_recv()
                first, _ = place[key]
                total = total + R[first : first + size, :].astype(jnp.float32)
        total = scale * total
        for d in range(count):
            half = total[(d // 2) * 8 : (d // 2) * 8 + 8, :]
            if d % 2:
                half = pltpu.roll(half, SHARED, 0)
            i = d + (Z if kind == "b" else 0)
            back_out[i] = pack(half).astype(jnp.bfloat16)
            owner = outer(ys_back[d], z, c) if kind == "b" else outer(y, zs_back[d], c)
            k = side * ring + d
            copy = remote(back_out.at[i], back.at[k], back_send.at[i], back_recv.at[k], (pod, owner))
            copy.start()
            returns.append(copy)

    def take_back(count):
        total = None
        for side in range(2):
            for d in range(count):
                k = side * ring + d
                remote(own_piece, back.at[k], back_send.at[0], back_recv.at[k], sibling).wait_recv()
                part = back[k].astype(jnp.float32)
                total = part if total is None else total + part
        back_sum[...] = total

    @pl.when(z_first)
    def _():
        take_back(Z)

    @pl.when(jnp.logical_not(z_first))
    def _():
        take_back(ring)

    lo, hi = back_sum[0:8, :], back_sum[8:16, :]
    spread = jnp.concatenate([lo, pltpu.roll(lo, SHARED, 0), hi, pltpu.roll(hi, SHARED, 0)], axis=1)
    up = nup[0:8, :] + jnp.where(upper_half(spread.shape), spread, 0.0)
    u = nu[0:8, :]
    radial = jnp.sum(u * up, axis=-1, keepdims=True)
    g = (ninv[0:8, :] * (up - u * radial)).astype(jnp.bfloat16)
    ng[0:8, :] = dot(g, nh[...], NT)
    stores[3].start()

    @pl.when(z_first)
    def _():
        for copy in piece_sends(True):
            copy.wait_send()

    @pl.when(jnp.logical_not(z_first))
    def _():
        for copy in piece_sends(False):
            copy.wait_send()

    for copy in list(gathers.values()) + list(reduces.values()) + returns:
        copy.wait_send()
    for copy in (sib_rec, sib_off, sib_rup, sib_loss):
        copy.wait_send()
    for copy in stores:
        copy.wait()


def write_out(loss_in, ng_in, eg_in, loss_out, ng_out, eg_out, loss, ng, eg, in_sem, out_sem):
    parts = 4
    rows = ng.shape[0] // parts
    moves = [(loss_in, loss, loss_out)]
    for src, held, dst in ((ng_in, ng, ng_out), (eg_in, eg, eg_out)):
        for j in range(parts):
            part = pl.ds(j * rows, rows)
            moves.append((src.at[part], held.at[part], dst.at[part]))
    loads = [pltpu.make_async_copy(src, held, in_sem.at[i]) for i, (src, held, _) in enumerate(moves)]
    stores = [pltpu.make_async_copy(held, dst, out_sem.at[i]) for i, (_, held, dst) in enumerate(moves)]
    for load in loads:
        load.start()
    for load, store in zip(loads, stores):
        load.wait()
        store.start()
    for store in stores:
        store.wait()


def per_device(n_loop, n_outer, note_feats, ehr_feats, note_head, ehr_head, logit_scale, bias_table, bias_index):
    pairs, width = note_feats.shape
    emb = note_head.shape[1]
    ring = n_outer // (Z * CORES)
    held = 2 * ring * BLOCK
    own = BLOCK + SHARED * ring
    others = ring + Z - 2
    bf16, f32 = jnp.bfloat16, jnp.float32
    vmem = pltpu.VMEM
    dma = pltpu.SemaphoreType.DMA
    hbm = pl.BlockSpec(memory_space=pltpu.HBM)
    outs = (
        jax.ShapeDtypeStruct((1, pairs), f32),
        jax.ShapeDtypeStruct((pairs, width), f32),
        jax.ShapeDtypeStruct((pairs, width), f32),
    )
    piece = (BLOCK, emb // 4)
    results = pl.pallas_call(
        functools.partial(kernel, n_loop, ring),
        out_shape=outs,
        in_specs=[hbm] * 7,
        out_specs=(hbm,) * 3,
        scratch_shapes=[
            vmem((pairs, width), bf16),
            vmem((pairs, width), bf16),
            vmem((width, emb), bf16),
            vmem((width, emb), bf16),
            pltpu.SMEM(logit_scale.shape, f32),
            pltpu.SMEM(bias_table.shape, f32),
            vmem((1, pairs), jnp.int32),
            vmem((pairs, emb), f32),
            vmem((pairs, emb), f32),
            vmem((pairs, 1), f32),
            vmem((pairs, 1), f32),
            vmem((pairs, emb), bf16),
            vmem((2 * pairs, emb), bf16),
            vmem((8, pairs), f32),
            vmem((8, pairs), f32),
            vmem((Z,) + piece, bf16),
            vmem((ring,) + piece, bf16),
            vmem(piece, bf16),
            vmem((held, emb), bf16),
            vmem((own, emb), f32),
            vmem((held, emb), bf16),
            vmem((held, emb), bf16),
            vmem((Z + ring,) + piece, bf16),
            vmem((2 * ring,) + piece, bf16),
            vmem(piece, f32),
            vmem((held, 2 * pairs), bf16),
            vmem((pairs, pairs), bf16),
            vmem((8, 2 * pairs), f32),
            vmem((8, pairs), f32),
            vmem((8, pairs), f32),
            vmem((pairs, emb), f32),
            vmem((pairs, emb), f32),
            vmem((pairs, emb), f32),
            vmem((pairs, emb), f32),
            vmem((pairs, emb), bf16),
            vmem((pairs, width), f32),
            vmem((pairs, width), f32),
            vmem((1, pairs), f32),
            dma((7,)),
            dma((4,)),
            dma((2 * ring,)),
            dma((Z,)),
            dma((ring,)),
            dma((others,)),
            dma((others,)),
            dma((others,)),
            dma((others,)),
            dma((Z + ring,)),
            dma((2 * ring,)),
            dma((4,)),
            dma((4,)),
        ],
        compiler_params=pltpu.CompilerParams(
            collective_id=0, has_side_effects=True, vmem_limit_bytes=56 * 1024 * 1024
        ),
    )(note_feats, ehr_feats, note_head, ehr_head, logit_scale, bias_table, bias_index.reshape(1, pairs))
    loss, note_grad, ehr_grad = pl.pallas_call(
        write_out,
        out_shape=outs,
        in_specs=[hbm] * 3,
        out_specs=(hbm,) * 3,
        scratch_shapes=[vmem(out.shape, f32) for out in outs] + [dma((9,)), dma((9,))],
        compiler_params=pltpu.CompilerParams(vmem_limit_bytes=62 * 1024 * 1024),
    )(*results)
    return loss.reshape(pairs), note_grad, ehr_grad


def solution(mesh):
    return jax.shard_map(
        functools.partial(per_device, mesh.shape["loop"], mesh.shape["outer"]),
        mesh=mesh,
        in_specs=(
            P(("loop", "outer"), None),
            P(("loop", "outer"), None),
            P(),
            P(),
            P(),
            P(),
            P(("loop", "outer")),
        ),
        out_specs=(P(("loop", "outer")), P(("loop", "outer"), None), P(("loop", "outer"), None)),
        check_vma=False,
    )
```

```python
import functools

import jax
import jax.numpy as jnp
from jax import lax
from jax.experimental import pallas as pl
from jax.experimental.pallas import tpu as pltpu
from jax.sharding import PartitionSpec as P

SHARED = 4
Z = 4
CORES = 2
X = 4
HEAD_PARTS = 4
BLOCK = SHARED * Z
MESH = pl.DeviceIdType.MESH
NT = (((1,), (1,)), ((), ()))
TN = (((0,), (0,)), ((), ()))


def dot(a, b, dims=(((1,), (0,)), ((), ()))):
    return lax.dot_general(a, b, dims, preferred_element_type=jnp.float32)


def terms(margins):
    t = jnp.exp(-jnp.abs(margins))
    r = 1.0 / (1.0 + t)
    return jnp.maximum(margins, 0.0) + jnp.log1p(t), jnp.where(margins >= 0.0, r, t * r)


def upper_half(shape):
    return lax.broadcasted_iota(jnp.int32, shape, 0) < SHARED


def pack(rows):
    w = rows.shape[1] // 4
    c = [rows[:, q * w : (q + 1) * w] for q in range(4)]
    up = upper_half(c[0].shape)
    lo = jnp.where(up, c[0], pltpu.roll(c[1], SHARED, 0))
    hi = jnp.where(up, c[2], pltpu.roll(c[3], SHARED, 0))
    return jnp.concatenate([lo, hi], axis=0)


def unpack_pair(first, second):
    up = upper_half((8, first.shape[1]))
    out = []
    for half in range(2):
        a, b = first[half * 8 : half * 8 + 8], second[half * 8 : half * 8 + 8]
        out.append(jnp.where(up, a, pltpu.roll(b, SHARED, 0)))
        out.append(jnp.where(up, pltpu.roll(a, SHARED, 0), b))
    return jnp.concatenate(out, axis=1)


def kernel(
    n_loop, ring,
    nf_hbm, ef_hbm, nh_hbm, eh_hbm, scale_hbm, table_hbm, index_hbm,
    loss_ref, ng, eg,
    nf, ef, nh, eh, scale_ref, table_ref, index_ref, nu, ru, ninv, rinv, ne, re, off, off_out,
    pieces_a, pieces_b, own_piece, W, G, S, R, held_a, own_a, sent_a, came_a, back_out, back, back_sum,
    slopes, local_slopes,
    lossacc, loss_out, loss_in, rup, rup_out, rup_in, nup, pre,
    load_sem, piece_send, recv_a, recv_b, ag_send, ag_recv, rs_send, rs_recv,
    fwd_send, fwd_recv, sum_send, sum_recv,
    back_send, back_recv, sib_send, sib_recv,
):
    pairs, width = nf.shape
    tile = min(256, width)
    tiles = width // tile
    l, o = lax.axis_index("loop"), lax.axis_index("outer")
    c, z, y = lax.rem(o, CORES), lax.rem(o // CORES, Z), o // (CORES * Z)
    x = lax.rem(l, X)
    z_first = lax.rem((x + 1) // 2, 2) == 0
    side_a = x // 2
    side_b = 1 - side_a
    pod_a = lax.rem(l + n_loop - 1 + 2 * side_a, n_loop)
    pod_b = lax.rem(l + n_loop + 1 - 2 * side_a, n_loop)

    def outer(yy, zz, cc):
        return (yy * Z + zz) * CORES + cc

    below, above = lax.rem(l + n_loop - 1, n_loop), lax.rem(l + 1, n_loop)
    ys = [lax.rem(y + d, ring) for d in range(ring)]
    zs = [lax.rem(z + d, Z) for d in range(Z)]
    ys_back = [lax.rem(y + ring - d, ring) for d in range(ring)]
    zs_back = [lax.rem(z + Z - d, Z) for d in range(Z)]
    sibling = (l, outer(y, z, 1 - c))

    barrier = pltpu.get_barrier_semaphore()
    partners = [sibling]
    partners += [(l, outer(yy, z, c)) for yy in ys[1:]] + [(l, outer(y, zz, c)) for zz in zs[1:]]
    for pod in (below, above):
        partners += [(pod, outer(yy, z, c)) for yy in ys] + [(pod, outer(y, zz, c)) for zz in zs[1:]]
    for partner in partners:
        pl.semaphore_signal(barrier, inc=1, device_id=partner, device_id_type=MESH)

    top_rows, deep = pl.ds(0, 16), nh.shape[0] // HEAD_PARTS
    other_rows = pl.ds(16, pairs - 16)
    moves = [(nf_hbm.at[top_rows], nf.at[top_rows])]
    for j in range(HEAD_PARTS):
        part = pl.ds(j * deep, deep)
        moves.append((nh_hbm.at[part], nh.at[part]))
    moves += [
        (nf_hbm.at[other_rows], nf.at[other_rows]), (eh_hbm, eh), (ef_hbm, ef),
        (scale_hbm, scale_ref), (table_hbm, table_ref), (index_hbm, index_ref),
    ]
    loads = [pltpu.make_async_copy(src, dst, load_sem.at[i]) for i, (src, dst) in enumerate(moves)]
    for load in loads:
        load.start()

    def remote(src, dst, send, recv, device):
        return pltpu.make_async_remote_copy(
            src_ref=src, dst_ref=dst, send_sem=send, recv_sem=recv, device_id=device, device_id_type=MESH
        )

    def project(feats, head, unit):
        def step(j, carry):
            cols = pl.ds(pl.multiple_of(j * tile, tile), tile)
            unit[:, cols] = dot(feats[...], head[:, cols])
            return carry

        lax.fori_loop(0, tiles, step, 0)

    def normalise(unit, inverse, emb):
        step_rows = min(64, pairs)

        def step(j, carry):
            rows = pl.ds(pl.multiple_of(j * step_rows, step_rows), step_rows)
            p = unit[rows, :]
            inv = lax.rsqrt(jnp.sum(p * p, axis=-1, keepdims=True) + 1e-06)
            u = p * inv
            inverse[rows, :] = inv
            unit[rows, :] = u
            emb[rows, :] = u.astype(jnp.bfloat16)
            return carry

        lax.fori_loop(0, pairs // step_rows, step, 0)

    for load in loads[: 2 + HEAD_PARTS]:
        load.wait()
    project(nf, nh, nu)
    top = nu[0:8, :]
    top = top * lax.rsqrt(jnp.sum(top * top, axis=-1, keepdims=True) + 1e-06)
    own_piece[...] = pack(top).astype(jnp.bfloat16)
    pl.semaphore_wait(barrier, len(partners))

    def piece_sends(along_z):
        copies = []
        for side, pod in enumerate((above, below)):
            for d in range(Z if along_z else ring):
                device = (pod, outer(y, zs[d], c) if along_z else outer(ys[d], z, c))
                landing, recv = (pieces_a, recv_a) if along_z else (pieces_b, recv_b)
                copies.append(
                    remote(own_piece, landing.at[d], piece_send.at[side * ring + d], recv.at[d], device)
                )
        return copies

    @pl.when(z_first)
    def _():
        for copy in piece_sends(True):
            copy.start()

    @pl.when(jnp.logical_not(z_first))
    def _():
        for copy in piece_sends(False):
            copy.start()

    normalise(nu, ninv, ne)

    for load in loads[2 + HEAD_PARTS :]:
        load.wait()
    project(ef, eh, ru)
    normalise(ru, rinv, re.at[pl.ds(0, pairs)])
    index = index_ref[...]
    offsets = jnp.zeros(index.shape, jnp.float32)
    for k in range(table_ref.shape[0]):
        offsets = jnp.where(index == k, table_ref[k], offsets)
    off_out[...] = jnp.broadcast_to(offsets, off_out.shape)
    sib_rec = remote(re.at[pl.ds(0, pairs)], re.at[pl.ds(pairs, pairs)], sib_send.at[0], sib_recv.at[0], sibling)
    sib_off = remote(off_out, off, sib_send.at[1], sib_recv.at[1], sibling)
    sib_rec.start()
    sib_off.start()
    scale = scale_ref[0]

    size = SHARED * ring
    far_first = sorted(range(1, ring), key=lambda d: -min(d, ring - d))

    def rows_b(d):
        return pl.ds(size * (Z + d), size)

    def forward(p, d):
        i = p * ring + d
        return remote(pieces_a.at[p], held_a.at[i], fwd_send.at[i], fwd_recv.at[i], (l, outer(ys[d], z, c)))

    def sum_a(p, d):
        i = p * ring + d
        return remote(sent_a.at[i], came_a.at[i], sum_send.at[i], sum_recv.at[i], (l, outer(ys_back[d], z, c)))

    forwards = {(p, d): forward(p, d) for p in range(Z) for d in far_first}
    sums_a = {(p, d): sum_a(p, d) for p in range(Z) for d in far_first}
    gathers, reduces = {}, {}
    for d in range(1, Z):
        gathers[d] = remote(
            W.at[rows_b(0)], W.at[rows_b(d)], ag_send.at[d], ag_recv.at[d], (l, outer(y, zs[d], c))
        )
        reduces[d] = remote(
            S.at[pl.ds(size * d, size)], R.at[pl.ds(size * d, size)], rs_send.at[d], rs_recv.at[d],
            (l, outer(y, zs_back[d], c)),
        )

    def unpacked(packed):
        return jnp.concatenate([unpack_pair(packed[d], packed[d + 1]) for d in range(0, len(packed), 2)], axis=0)

    for p in range(Z):
        remote(own_piece, pieces_a.at[p], piece_send.at[0], recv_a.at[p], sibling).wait_recv()
        for d in far_first:
            forwards[p, d].start()
    for d in range(ring):
        remote(own_piece, pieces_b.at[d], piece_send.at[0], recv_b.at[d], sibling).wait_recv()
    W[rows_b(0), :] = unpacked([pieces_b[d].astype(jnp.float32) for d in range(ring)]).astype(jnp.bfloat16)
    for d in (2, 1, 3):
        gathers[d].start()

    sims = dot(ne[...], re[0:pairs, :], NT)
    logits = scale * sims + offsets
    positive = lax.broadcasted_iota(jnp.int32, logits.shape, 0) == lax.broadcasted_iota(jnp.int32, logits.shape, 1)
    softplus, sigmoid = terms(jnp.where(positive, -logits, logits))
    local_slopes[...] = jnp.where(positive, -sigmoid, sigmoid).astype(jnp.bfloat16)
    lossacc[:, 0:pairs] = jnp.sum(softplus.reshape(pairs // 8, 8, pairs), axis=0)
    lossacc[:, pairs:] = jnp.zeros((8, pairs), jnp.float32)

    def back_grad(head, out):
        def step(j, carry):
            cols = pl.ds(pl.multiple_of(j * tile, tile), tile)
            out[:, cols] = dot(pre[...], head[cols, :], NT)
            return carry

        lax.fori_loop(0, tiles, step, 0)

    def pre_grads(unit, inverse, upstream):
        step_rows = min(64, pairs)

        def step(j, carry):
            rows = pl.ds(pl.multiple_of(j * step_rows, step_rows), step_rows)
            u, up = unit[rows, :], upstream(rows)
            radial = jnp.sum(u * up, axis=-1, keepdims=True)
            pre[rows, :] = (inverse[rows, :] * (up - u * radial)).astype(jnp.bfloat16)
            return carry

        lax.fori_loop(0, pairs // step_rows, step, 0)

    sib_off.wait_recv()
    sib_rec.wait_recv()
    all_offsets = jnp.concatenate([off_out[0:1, :], off[0:1, :]], axis=1)

    def work(start):
        rows = slice(start, start + size)
        logits = scale * dot(W[rows, :], re[...], NT) + all_offsets
        softplus, sigmoid = terms(logits)
        lossacc[...] += jnp.sum(softplus.reshape(size // 8, 8, 2 * pairs), axis=0)
        s = sigmoid.astype(jnp.bfloat16)
        slopes[rows, :] = s
        return dot(s, re[...])

    def work_b(d):
        gathers[d].wait_recv()
        S[pl.ds(size * d, size), :] = work(size * (Z + d)).astype(jnp.bfloat16)
        reduces[d].start()

    def work_a(p):
        for d in far_first:
            forwards[p, d].wait_recv()
        packed = [pieces_a[p]] + [held_a[p * ring + d] for d in range(1, ring)]
        W[size * p : size * (p + 1), :] = unpacked([q.astype(jnp.float32) for q in packed]).astype(jnp.bfloat16)
        grads = work(size * p)
        for d in [0] + far_first:
            half = grads[(d // 2) * 8 : (d // 2) * 8 + 8, :]
            if d % 2:
                half = pltpu.roll(half, SHARED, 0)
            if d == 0:
                own_a[p] = pack(half)
            else:
                sent_a[p * ring + d] = pack(half).astype(jnp.bfloat16)
                sums_a[p, d].start()

    G[...] = work(size * Z)

    def upstream_notes(j, carry):
        cols = pl.ds(pl.multiple_of(j * tile, tile), tile)
        nup[:, cols] = scale * dot(local_slopes[...], re[0:pairs, cols])
        return carry

    lax.fori_loop(0, tiles, upstream_notes, 0)
    pre_grads(nu, ninv, lambda rows: nup[rows, :])
    back_grad(nh, ng)
    work_a(0)
    work_b(1)
    work_a(1)
    work_b(3)
    work_a(2)
    work_b(2)
    work_a(3)

    def upstream_sibling(j, carry):
        cols = pl.ds(pl.multiple_of(j * tile, tile), tile)
        rup_out[:, cols] = dot(slopes[:, pairs:], W[:, cols], TN)
        return carry

    def upstream_own(j, carry):
        cols = pl.ds(pl.multiple_of(j * tile, tile), tile)
        rup[:, cols] = dot(slopes[:, 0:pairs], W[:, cols], TN) + dot(local_slopes[...], ne[:, cols], TN)
        return carry

    lax.fori_loop(0, tiles, upstream_sibling, 0)
    loss_out[...] = lossacc[:, pairs:]
    sib_rup = remote(rup_out, rup_in, sib_send.at[2], sib_recv.at[2], sibling)
    sib_loss = remote(loss_out, loss_in, sib_send.at[3], sib_recv.at[3], sibling)
    sib_rup.start()
    sib_loss.start()
    lax.fori_loop(0, tiles, upstream_own, 0)

    returns = []

    def give(i, d, kind):
        owner = outer(ys_back[d], z, c) if kind == "b" else outer(y, zs_back[d], c)
        pod, side = (pod_b, side_b) if kind == "b" else (pod_a, side_a)
        k = side * ring + d
        copy = remote(back_out.at[i], back.at[k], back_send.at[i], back_recv.at[k], (pod, owner))
        copy.start()
        returns.append(copy)

    def return_a(p):
        total = own_a[p]
        for d in far_first:
            sums_a[p, d].wait_recv()
            total = total + came_a[p * ring + d].astype(jnp.float32)
        back_out[p] = (scale * total).astype(jnp.bfloat16)
        give(p, p, "a")

    def return_b():
        total = G[...]
        for d in range(1, Z):
            reduces[d].wait_recv()
            total = total + R[pl.ds(size * d, size), :].astype(jnp.float32)
        total = scale * total
        for d in range(ring):
            half = total[(d // 2) * 8 : (d // 2) * 8 + 8, :]
            if d % 2:
                half = pltpu.roll(half, SHARED, 0)
            back_out[Z + d] = pack(half).astype(jnp.bfloat16)
            give(Z + d, d, "b")

    return_a(0)
    return_a(1)
    return_b()
    return_a(2)
    return_a(3)

    sib_rup.wait_recv()
    sib_loss.wait_recv()
    loss = jnp.sum(lossacc[:, 0:pairs] + loss_in[...], axis=0, keepdims=True)
    loss_ref[...] = loss * (1.0 / (pairs + ring * Z * CORES * SHARED * 2))
    pre_grads(ru, rinv, lambda rows: scale * (rup[rows, :] + rup_in[rows, :]))
    back_grad(eh, eg)

    def take_back(count):
        total = None
        for side in range(2):
            for d in range(count):
                k = side * ring + d
                remote(own_piece, back.at[k], back_send.at[0], back_recv.at[k], sibling).wait_recv()
                part = back[k].astype(jnp.float32)
                total = part if total is None else total + part
        back_sum[...] = total

    @pl.when(z_first)
    def _():
        take_back(Z)

    @pl.when(jnp.logical_not(z_first))
    def _():
        take_back(ring)

    lo, hi = back_sum[0:8, :], back_sum[8:16, :]
    spread = jnp.concatenate([lo, pltpu.roll(lo, SHARED, 0), hi, pltpu.roll(hi, SHARED, 0)], axis=1)
    up = nup[0:8, :] + jnp.where(upper_half(spread.shape), spread, 0.0)
    u = nu[0:8, :]
    radial = jnp.sum(u * up, axis=-1, keepdims=True)
    g = (ninv[0:8, :] * (up - u * radial)).astype(jnp.bfloat16)
    ng[0:8, :] = dot(g, nh[...], NT)

    @pl.when(z_first)
    def _():
        for copy in piece_sends(True):
            copy.wait_send()

    @pl.when(jnp.logical_not(z_first))
    def _():
        for copy in piece_sends(False):
            copy.wait_send()

    rings = list(forwards.values()) + list(sums_a.values())
    for copy in rings + list(gathers.values()) + list(reduces.values()) + returns:
        copy.wait_send()
    for copy in (sib_rec, sib_off, sib_rup, sib_loss):
        copy.wait_send()


def write_out(loss, ng, eg, loss_out, ng_out, eg_out, sem):
    copies = [
        pltpu.make_async_copy(src, dst, sem.at[i])
        for i, (src, dst) in enumerate(((ng, ng_out), (eg, eg_out), (loss, loss_out)))
    ]
    for copy in copies:
        copy.start()
    for copy in copies:
        copy.wait()


def in_hbm(a):
    return pltpu.with_memory_space_constraint(a, pltpu.HBM)


def per_device(n_loop, n_outer, note_feats, ehr_feats, note_head, ehr_head, logit_scale, bias_table, bias_index):
    pairs, width = note_feats.shape
    emb = note_head.shape[1]
    ring = n_outer // (Z * CORES)
    held = 2 * ring * BLOCK
    own = SHARED * ring
    bf16, f32 = jnp.bfloat16, jnp.float32
    vmem = pltpu.VMEM
    dma = pltpu.SemaphoreType.DMA
    hbm = pl.BlockSpec(memory_space=pltpu.HBM)
    whole = pl.BlockSpec(memory_space=pltpu.VMEM)
    outs = (
        jax.ShapeDtypeStruct((1, pairs), f32),
        jax.ShapeDtypeStruct((pairs, width), f32),
        jax.ShapeDtypeStruct((pairs, width), f32),
    )
    piece = (BLOCK, emb // 4)
    results = pl.pallas_call(
        functools.partial(kernel, n_loop, ring),
        out_shape=tuple(vmem(out.shape, f32) for out in outs),
        in_specs=[hbm] * 7,
        out_specs=(whole,) * 3,
        scratch_shapes=[
            vmem((pairs, width), bf16),
            vmem((pairs, width), bf16),
            vmem((width, emb), bf16),
            vmem((width, emb), bf16),
            pltpu.SMEM(logit_scale.shape, f32),
            pltpu.SMEM(bias_table.shape, f32),
            vmem((1, pairs), jnp.int32),
            vmem((pairs, emb), f32),
            vmem((pairs, emb), f32),
            vmem((pairs, 1), f32),
            vmem((pairs, 1), f32),
            vmem((pairs, emb), bf16),
            vmem((2 * pairs, emb), bf16),
            vmem((8, pairs), f32),
            vmem((8, pairs), f32),
            vmem((Z,) + piece, bf16),
            vmem((ring,) + piece, bf16),
            vmem(piece, bf16),
            vmem((held, emb), bf16),
            vmem((own, emb), f32),
            vmem((held // 2, emb), bf16),
            vmem((held // 2, emb), bf16),
            vmem((Z * ring,) + piece, bf16),
            vmem((Z,) + piece, f32),
            vmem((Z * ring,) + piece, bf16),
            vmem((Z * ring,) + piece, bf16),
            vmem((Z + ring,) + piece, bf16),
            vmem((2 * ring,) + piece, bf16),
            vmem(piece, f32),
            vmem((held, 2 * pairs), bf16),
            vmem((pairs, pairs), bf16),
            vmem((8, 2 * pairs), f32),
            vmem((8, pairs), f32),
            vmem((8, pairs), f32),
            vmem((pairs, emb), f32),
            vmem((pairs, emb), f32),
            vmem((pairs, emb), f32),
            vmem((pairs, emb), f32),
            vmem((pairs, emb), bf16),
            dma((7 + HEAD_PARTS,)),
            dma((2 * ring,)),
            dma((Z,)),
            dma((ring,)),
            dma((Z,)),
            dma((Z,)),
            dma((Z,)),
            dma((Z,)),
            dma((Z * ring,)),
            dma((Z * ring,)),
            dma((Z * ring,)),
            dma((Z * ring,)),
            dma((Z + ring,)),
            dma((2 * ring,)),
            dma((4,)),
            dma((4,)),
        ],
        compiler_params=pltpu.CompilerParams(
            collective_id=0, has_side_effects=True, vmem_limit_bytes=48 * 1024 * 1024
        ),
    )(
        in_hbm(note_feats), in_hbm(ehr_feats), in_hbm(note_head), in_hbm(ehr_head), logit_scale, in_hbm(bias_table),
        in_hbm(bias_index.reshape(1, pairs)),
    )
    loss, note_grad, ehr_grad = pl.pallas_call(
        write_out,
        out_shape=outs,
        in_specs=[whole] * 3,
        out_specs=(hbm,) * 3,
        scratch_shapes=[dma((3,))],
        compiler_params=pltpu.CompilerParams(vmem_limit_bytes=4 * 1024 * 1024),
    )(*results)
    return loss.reshape(pairs), note_grad, ehr_grad


def solution(mesh):
    return jax.shard_map(
        functools.partial(per_device, mesh.shape["loop"], mesh.shape["outer"]),
        mesh=mesh,
        in_specs=(
            P(("loop", "outer"), None),
            P(("loop", "outer"), None),
            P(),
            P(),
            P(),
            P(),
            P(("loop", "outer")),
        ),
        out_specs=(P(("loop", "outer")), P(("loop", "outer"), None), P(("loop", "outer"), None)),
        check_vma=False,
    )
```

```python
import functools

import jax
import jax.numpy as jnp
from jax import lax
from jax.experimental import pallas as pl
from jax.experimental.pallas import tpu as pltpu
from jax.sharding import PartitionSpec as P

SHARED = 4
Z = 4
CORES = 2
X = 4
HEAD_PARTS = 4
BLOCK = SHARED * Z
MESH = pl.DeviceIdType.MESH
NT = (((1,), (1,)), ((), ()))
TN = (((0,), (0,)), ((), ()))


def dot(a, b, dims=(((1,), (0,)), ((), ()))):
    return lax.dot_general(a, b, dims, preferred_element_type=jnp.float32)


def terms(margins):
    t = jnp.exp(-jnp.abs(margins))
    r = 1.0 / (1.0 + t)
    return jnp.maximum(margins, 0.0) + jnp.log1p(t), jnp.where(margins >= 0.0, r, t * r)


def upper_half(shape):
    return lax.broadcasted_iota(jnp.int32, shape, 0) < SHARED


def pack(rows):
    w = rows.shape[1] // 4
    c = [rows[:, q * w : (q + 1) * w] for q in range(4)]
    up = upper_half(c[0].shape)
    lo = jnp.where(up, c[0], pltpu.roll(c[1], SHARED, 0))
    hi = jnp.where(up, c[2], pltpu.roll(c[3], SHARED, 0))
    return jnp.concatenate([lo, hi], axis=0)


def unpack_pair(first, second):
    up = upper_half((8, first.shape[1]))
    out = []
    for half in range(2):
        a, b = first[half * 8 : half * 8 + 8], second[half * 8 : half * 8 + 8]
        out.append(jnp.where(up, a, pltpu.roll(b, SHARED, 0)))
        out.append(jnp.where(up, pltpu.roll(a, SHARED, 0), b))
    return jnp.concatenate(out, axis=1)


def kernel(
    n_loop, ring,
    nf_hbm, ef_hbm, nh_hbm, eh_hbm, scale_hbm, table_hbm, index_hbm,
    loss_ref, ng, eg,
    nf, ef, nh, eh, scale_ref, table_ref, index_ref, nu, ru, ninv, rinv, ne, re, off, off_out,
    pieces_a, pieces_b, own_piece, W, G, S, R, held_a, own_a, sent_a, came_a, back_out, back, back_sum,
    slopes, local_slopes,
    lossacc, loss_out, loss_in, rup, rup_out, rup_in, nup, pre,
    load_sem, piece_send, recv_a, recv_b, ag_send, ag_recv, rs_send, rs_recv,
    fwd_send, fwd_recv, sum_send, sum_recv,
    back_send, back_recv, sib_send, sib_recv,
):
    pairs, width = nf.shape
    tile = min(256, width)
    tiles = width // tile
    l, o = lax.axis_index("loop"), lax.axis_index("outer")
    c, z, y = lax.rem(o, CORES), lax.rem(o // CORES, Z), o // (CORES * Z)
    x = lax.rem(l, X)
    y_first = lax.rem((x + 1) // 2, 2)
    z_first = y_first == 0
    side_a = x // 2
    side_b = 1 - side_a
    pod_a = lax.rem(l + n_loop - 1 + 2 * side_a, n_loop)
    pod_b = lax.rem(l + n_loop + 1 - 2 * side_a, n_loop)

    def outer(yy, zz, cc):
        return (yy * Z + zz) * CORES + cc

    below, above = lax.rem(l + n_loop - 1, n_loop), lax.rem(l + 1, n_loop)
    ys = [lax.rem(y + d, ring) for d in range(ring)]
    zs = [lax.rem(z + d, Z) for d in range(Z)]
    ys_back = [lax.rem(y + ring - d, ring) for d in range(ring)]
    zs_back = [lax.rem(z + Z - d, Z) for d in range(Z)]
    sibling = (l, outer(y, z, 1 - c))

    barrier = pltpu.get_barrier_semaphore()
    partners = [(pod_a, outer(y, zz, c)) for zz in zs] + [(pod_b, outer(yy, z, c)) for yy in ys]
    partners += [(l, outer(yy, z, c)) for yy in ys[1:]] + [(l, outer(y, zz, c)) for zz in zs[1:]] + [sibling]
    also = {True: [(pod_b, outer(y, zz, c)) for zz in zs[1:]], False: [(pod_a, outer(yy, z, c)) for yy in ys[1:]]}

    def greet(devices):
        for device in devices:
            pl.semaphore_signal(barrier, inc=1, device_id=device, device_id_type=MESH)

    greet(partners)

    @pl.when(z_first)
    def _():
        greet(also[True])

    @pl.when(jnp.logical_not(z_first))
    def _():
        greet(also[False])

    top_rows, deep = pl.ds(0, 16), nh.shape[0] // HEAD_PARTS
    other_rows = pl.ds(16, pairs - 16)
    moves = [(nf_hbm.at[top_rows], nf.at[top_rows])]
    for j in range(HEAD_PARTS):
        part = pl.ds(j * deep, deep)
        moves.append((nh_hbm.at[part], nh.at[part]))
    moves += [
        (nf_hbm.at[other_rows], nf.at[other_rows]), (eh_hbm, eh), (ef_hbm, ef),
        (scale_hbm, scale_ref), (table_hbm, table_ref), (index_hbm, index_ref),
    ]
    loads = [pltpu.make_async_copy(src, dst, load_sem.at[i]) for i, (src, dst) in enumerate(moves)]
    for load in loads:
        load.start()

    def remote(src, dst, send, recv, device):
        return pltpu.make_async_remote_copy(
            src_ref=src, dst_ref=dst, send_sem=send, recv_sem=recv, device_id=device, device_id_type=MESH
        )

    def project(feats, head, unit):
        def step(j, carry):
            cols = pl.ds(pl.multiple_of(j * tile, tile), tile)
            unit[:, cols] = dot(feats[...], head[:, cols])
            return carry

        lax.fori_loop(0, tiles, step, 0)

    def normalise(unit, inverse, emb):
        step_rows = min(64, pairs)

        def step(j, carry):
            rows = pl.ds(pl.multiple_of(j * step_rows, step_rows), step_rows)
            p = unit[rows, :]
            inv = lax.rsqrt(jnp.sum(p * p, axis=-1, keepdims=True) + 1e-06)
            u = p * inv
            inverse[rows, :] = inv
            unit[rows, :] = u
            emb[rows, :] = u.astype(jnp.bfloat16)
            return carry

        lax.fori_loop(0, pairs // step_rows, step, 0)

    for load in loads[: 2 + HEAD_PARTS]:
        load.wait()
    project(nf, nh, nu)
    top = nu[0:8, :]
    top = top * lax.rsqrt(jnp.sum(top * top, axis=-1, keepdims=True) + 1e-06)
    own_piece[...] = pack(top).astype(jnp.bfloat16)
    pl.semaphore_wait(barrier, len(partners) + len(also[True]) + (len(also[False]) - len(also[True])) * y_first)

    def piece_sends(along_z):
        copies = []
        for side, pod in enumerate((above, below)):
            for d in range(Z if along_z else ring):
                device = (pod, outer(y, zs[d], c) if along_z else outer(ys[d], z, c))
                landing, recv = (pieces_a, recv_a) if along_z else (pieces_b, recv_b)
                copies.append(
                    remote(own_piece, landing.at[d], piece_send.at[side * ring + d], recv.at[d], device)
                )
        return copies

    @pl.when(z_first)
    def _():
        for copy in piece_sends(True):
            copy.start()

    @pl.when(jnp.logical_not(z_first))
    def _():
        for copy in piece_sends(False):
            copy.start()

    normalise(nu, ninv, ne)

    for load in loads[2 + HEAD_PARTS :]:
        load.wait()
    project(ef, eh, ru)
    normalise(ru, rinv, re.at[pl.ds(0, pairs)])
    index = index_ref[...]
    offsets = jnp.zeros(index.shape, jnp.float32)
    for k in range(table_ref.shape[0]):
        offsets = jnp.where(index == k, table_ref[k], offsets)
    off_out[...] = jnp.broadcast_to(offsets, off_out.shape)
    sib_rec = remote(re.at[pl.ds(0, pairs)], re.at[pl.ds(pairs, pairs)], sib_send.at[0], sib_recv.at[0], sibling)
    sib_off = remote(off_out, off, sib_send.at[1], sib_recv.at[1], sibling)
    sib_rec.start()
    sib_off.start()
    scale = scale_ref[0]

    size = SHARED * ring
    far_first = sorted(range(1, ring), key=lambda d: -min(d, ring - d))

    def rows_b(d):
        return pl.ds(size * (Z + d), size)

    def forward(p, d):
        i = p * ring + d
        return remote(pieces_a.at[p], held_a.at[i], fwd_send.at[i], fwd_recv.at[i], (l, outer(ys[d], z, c)))

    def sum_a(p, d):
        i = p * ring + d
        return remote(sent_a.at[i], came_a.at[i], sum_send.at[i], sum_recv.at[i], (l, outer(ys_back[d], z, c)))

    forwards = {(p, d): forward(p, d) for p in range(Z) for d in far_first}
    sums_a = {(p, d): sum_a(p, d) for p in range(Z) for d in far_first}
    gathers, reduces = {}, {}
    for d in range(1, Z):
        gathers[d] = remote(
            W.at[rows_b(0)], W.at[rows_b(d)], ag_send.at[d], ag_recv.at[d], (l, outer(y, zs[d], c))
        )
        reduces[d] = remote(
            S.at[pl.ds(size * d, size)], R.at[pl.ds(size * d, size)], rs_send.at[d], rs_recv.at[d],
            (l, outer(y, zs_back[d], c)),
        )

    def unpacked(packed):
        return jnp.concatenate([unpack_pair(packed[d], packed[d + 1]) for d in range(0, len(packed), 2)], axis=0)

    for p in range(Z):
        remote(own_piece, pieces_a.at[p], piece_send.at[0], recv_a.at[p], sibling).wait_recv()
        for d in far_first:
            forwards[p, d].start()
    for d in range(ring):
        remote(own_piece, pieces_b.at[d], piece_send.at[0], recv_b.at[d], sibling).wait_recv()
    W[rows_b(0), :] = unpacked([pieces_b[d].astype(jnp.float32) for d in range(ring)]).astype(jnp.bfloat16)
    for d in (2, 1, 3):
        gathers[d].start()

    sims = dot(ne[...], re[0:pairs, :], NT)
    logits = scale * sims + offsets
    positive = lax.broadcasted_iota(jnp.int32, logits.shape, 0) == lax.broadcasted_iota(jnp.int32, logits.shape, 1)
    softplus, sigmoid = terms(jnp.where(positive, -logits, logits))
    local_slopes[...] = jnp.where(positive, -sigmoid, sigmoid).astype(jnp.bfloat16)
    lossacc[:, 0:pairs] = jnp.sum(softplus.reshape(pairs // 8, 8, pairs), axis=0)
    lossacc[:, pairs:] = jnp.zeros((8, pairs), jnp.float32)

    def back_grad(head, out):
        def step(j, carry):
            cols = pl.ds(pl.multiple_of(j * tile, tile), tile)
            out[:, cols] = dot(pre[...], head[cols, :], NT)
            return carry

        lax.fori_loop(0, tiles, step, 0)

    def pre_grads(unit, inverse, upstream):
        step_rows = min(64, pairs)

        def step(j, carry):
            rows = pl.ds(pl.multiple_of(j * step_rows, step_rows), step_rows)
            u, up = unit[rows, :], upstream(rows)
            radial = jnp.sum(u * up, axis=-1, keepdims=True)
            pre[rows, :] = (inverse[rows, :] * (up - u * radial)).astype(jnp.bfloat16)
            return carry

        lax.fori_loop(0, pairs // step_rows, step, 0)

    sib_off.wait_recv()
    sib_rec.wait_recv()
    all_offsets = jnp.concatenate([off_out[0:1, :], off[0:1, :]], axis=1)

    def work(start):
        rows = slice(start, start + size)
        logits = scale * dot(W[rows, :], re[...], NT) + all_offsets
        softplus, sigmoid = terms(logits)
        lossacc[...] += jnp.sum(softplus.reshape(size // 8, 8, 2 * pairs), axis=0)
        s = sigmoid.astype(jnp.bfloat16)
        slopes[rows, :] = s
        return dot(s, re[...])

    def work_b(d):
        gathers[d].wait_recv()
        S[pl.ds(size * d, size), :] = work(size * (Z + d)).astype(jnp.bfloat16)
        reduces[d].start()

    def work_a(p):
        for d in far_first:
            forwards[p, d].wait_recv()
        packed = [pieces_a[p]] + [held_a[p * ring + d] for d in range(1, ring)]
        W[size * p : size * (p + 1), :] = unpacked([q.astype(jnp.float32) for q in packed]).astype(jnp.bfloat16)
        grads = work(size * p)
        for d in [0] + far_first:
            half = grads[(d // 2) * 8 : (d // 2) * 8 + 8, :]
            if d % 2:
                half = pltpu.roll(half, SHARED, 0)
            if d == 0:
                own_a[p] = pack(half)
            else:
                sent_a[p * ring + d] = pack(half).astype(jnp.bfloat16)
                sums_a[p, d].start()

    G[...] = work(size * Z)

    def upstream_notes(j, carry):
        cols = pl.ds(pl.multiple_of(j * tile, tile), tile)
        nup[:, cols] = scale * dot(local_slopes[...], re[0:pairs, cols])
        return carry

    lax.fori_loop(0, tiles, upstream_notes, 0)
    pre_grads(nu, ninv, lambda rows: nup[rows, :])
    back_grad(nh, ng)
    work_a(0)
    work_b(1)
    work_a(1)
    work_b(3)
    work_a(2)
    work_b(2)
    work_a(3)

    def upstream_sibling(j, carry):
        cols = pl.ds(pl.multiple_of(j * tile, tile), tile)
        rup_out[:, cols] = dot(slopes[:, pairs:], W[:, cols], TN)
        return carry

    def upstream_own(j, carry):
        cols = pl.ds(pl.multiple_of(j * tile, tile), tile)
        rup[:, cols] = dot(slopes[:, 0:pairs], W[:, cols], TN) + dot(local_slopes[...], ne[:, cols], TN)
        return carry

    lax.fori_loop(0, tiles, upstream_sibling, 0)
    loss_out[...] = lossacc[:, pairs:]
    sib_rup = remote(rup_out, rup_in, sib_send.at[2], sib_recv.at[2], sibling)
    sib_loss = remote(loss_out, loss_in, sib_send.at[3], sib_recv.at[3], sibling)
    sib_rup.start()
    sib_loss.start()
    lax.fori_loop(0, tiles, upstream_own, 0)

    returns = []

    def give(i, d, kind):
        owner = outer(ys_back[d], z, c) if kind == "b" else outer(y, zs_back[d], c)
        pod, side = (pod_b, side_b) if kind == "b" else (pod_a, side_a)
        k = side * ring + d
        copy = remote(back_out.at[i], back.at[k], back_send.at[i], back_recv.at[k], (pod, owner))
        copy.start()
        returns.append(copy)

    def return_a(p):
        total = own_a[p]
        for d in far_first:
            sums_a[p, d].wait_recv()
            total = total + came_a[p * ring + d].astype(jnp.float32)
        back_out[p] = (scale * total).astype(jnp.bfloat16)
        give(p, p, "a")

    def return_b():
        total = G[...]
        for d in range(1, Z):
            reduces[d].wait_recv()
            total = total + R[pl.ds(size * d, size), :].astype(jnp.float32)
        total = scale * total
        for d in range(ring):
            half = total[(d // 2) * 8 : (d // 2) * 8 + 8, :]
            if d % 2:
                half = pltpu.roll(half, SHARED, 0)
            back_out[Z + d] = pack(half).astype(jnp.bfloat16)
            give(Z + d, d, "b")

    return_a(0)
    return_a(1)
    return_b()
    return_a(2)
    return_a(3)

    sib_rup.wait_recv()
    sib_loss.wait_recv()
    loss = jnp.sum(lossacc[:, 0:pairs] + loss_in[...], axis=0, keepdims=True)
    loss_ref[...] = loss * (1.0 / (pairs + ring * Z * CORES * SHARED * 2))
    pre_grads(ru, rinv, lambda rows: scale * (rup[rows, :] + rup_in[rows, :]))
    back_grad(eh, eg)

    def take_back(count):
        total = None
        for side in range(2):
            for d in range(count):
                k = side * ring + d
                remote(own_piece, back.at[k], back_send.at[0], back_recv.at[k], sibling).wait_recv()
                part = back[k].astype(jnp.float32)
                total = part if total is None else total + part
        back_sum[...] = total

    @pl.when(z_first)
    def _():
        take_back(Z)

    @pl.when(jnp.logical_not(z_first))
    def _():
        take_back(ring)

    lo, hi = back_sum[0:8, :], back_sum[8:16, :]
    spread = jnp.concatenate([lo, pltpu.roll(lo, SHARED, 0), hi, pltpu.roll(hi, SHARED, 0)], axis=1)
    up = nup[0:8, :] + jnp.where(upper_half(spread.shape), spread, 0.0)
    u = nu[0:8, :]
    radial = jnp.sum(u * up, axis=-1, keepdims=True)
    g = (ninv[0:8, :] * (up - u * radial)).astype(jnp.bfloat16)
    ng[0:8, :] = dot(g, nh[...], NT)

    @pl.when(z_first)
    def _():
        for copy in piece_sends(True):
            copy.wait_send()

    @pl.when(jnp.logical_not(z_first))
    def _():
        for copy in piece_sends(False):
            copy.wait_send()

    rings = list(forwards.values()) + list(sums_a.values())
    for copy in rings + list(gathers.values()) + list(reduces.values()) + returns:
        copy.wait_send()
    for copy in (sib_rec, sib_off, sib_rup, sib_loss):
        copy.wait_send()


def write_out(loss, ng, eg, loss_out, ng_out, eg_out, sem):
    copies = [
        pltpu.make_async_copy(src, dst, sem.at[i])
        for i, (src, dst) in enumerate(((ng, ng_out), (eg, eg_out), (loss, loss_out)))
    ]
    for copy in copies:
        copy.start()
    for copy in copies:
        copy.wait()


def in_hbm(a):
    return pltpu.with_memory_space_constraint(a, pltpu.HBM)


def per_device(n_loop, n_outer, note_feats, ehr_feats, note_head, ehr_head, logit_scale, bias_table, bias_index):
    pairs, width = note_feats.shape
    emb = note_head.shape[1]
    ring = n_outer // (Z * CORES)
    held = 2 * ring * BLOCK
    own = SHARED * ring
    bf16, f32 = jnp.bfloat16, jnp.float32
    vmem = pltpu.VMEM
    dma = pltpu.SemaphoreType.DMA
    hbm = pl.BlockSpec(memory_space=pltpu.HBM)
    whole = pl.BlockSpec(memory_space=pltpu.VMEM)
    outs = (
        jax.ShapeDtypeStruct((1, pairs), f32),
        jax.ShapeDtypeStruct((pairs, width), f32),
        jax.ShapeDtypeStruct((pairs, width), f32),
    )
    piece = (BLOCK, emb // 4)
    results = pl.pallas_call(
        functools.partial(kernel, n_loop, ring),
        out_shape=tuple(vmem(out.shape, f32) for out in outs),
        in_specs=[hbm] * 7,
        out_specs=(whole,) * 3,
        scratch_shapes=[
            vmem((pairs, width), bf16),
            vmem((pairs, width), bf16),
            vmem((width, emb), bf16),
            vmem((width, emb), bf16),
            pltpu.SMEM(logit_scale.shape, f32),
            pltpu.SMEM(bias_table.shape, f32),
            vmem((1, pairs), jnp.int32),
            vmem((pairs, emb), f32),
            vmem((pairs, emb), f32),
            vmem((pairs, 1), f32),
            vmem((pairs, 1), f32),
            vmem((pairs, emb), bf16),
            vmem((2 * pairs, emb), bf16),
            vmem((8, pairs), f32),
            vmem((8, pairs), f32),
            vmem((Z,) + piece, bf16),
            vmem((ring,) + piece, bf16),
            vmem(piece, bf16),
            vmem((held, emb), bf16),
            vmem((own, emb), f32),
            vmem((held // 2, emb), bf16),
            vmem((held // 2, emb), bf16),
            vmem((Z * ring,) + piece, bf16),
            vmem((Z,) + piece, f32),
            vmem((Z * ring,) + piece, bf16),
            vmem((Z * ring,) + piece, bf16),
            vmem((Z + ring,) + piece, bf16),
            vmem((2 * ring,) + piece, bf16),
            vmem(piece, f32),
            vmem((held, 2 * pairs), bf16),
            vmem((pairs, pairs), bf16),
            vmem((8, 2 * pairs), f32),
            vmem((8, pairs), f32),
            vmem((8, pairs), f32),
            vmem((pairs, emb), f32),
            vmem((pairs, emb), f32),
            vmem((pairs, emb), f32),
            vmem((pairs, emb), f32),
            vmem((pairs, emb), bf16),
            dma((7 + HEAD_PARTS,)),
            dma((2 * ring,)),
            dma((Z,)),
            dma((ring,)),
            dma((Z,)),
            dma((Z,)),
            dma((Z,)),
            dma((Z,)),
            dma((Z * ring,)),
            dma((Z * ring,)),
            dma((Z * ring,)),
            dma((Z * ring,)),
            dma((Z + ring,)),
            dma((2 * ring,)),
            dma((4,)),
            dma((4,)),
        ],
        compiler_params=pltpu.CompilerParams(
            collective_id=0, has_side_effects=True, vmem_limit_bytes=48 * 1024 * 1024
        ),
    )(
        in_hbm(note_feats), in_hbm(ehr_feats), in_hbm(note_head), in_hbm(ehr_head), logit_scale, in_hbm(bias_table),
        in_hbm(bias_index.reshape(1, pairs)),
    )
    loss, note_grad, ehr_grad = pl.pallas_call(
        write_out,
        out_shape=outs,
        in_specs=[whole] * 3,
        out_specs=(hbm,) * 3,
        scratch_shapes=[dma((3,))],
        compiler_params=pltpu.CompilerParams(vmem_limit_bytes=4 * 1024 * 1024),
    )(*results)
    return loss.reshape(pairs), note_grad, ehr_grad


def solution(mesh):
    return jax.shard_map(
        functools.partial(per_device, mesh.shape["loop"], mesh.shape["outer"]),
        mesh=mesh,
        in_specs=(
            P(("loop", "outer"), None),
            P(("loop", "outer"), None),
            P(),
            P(),
            P(),
            P(),
            P(("loop", "outer")),
        ),
        out_specs=(P(("loop", "outer")), P(("loop", "outer"), None), P(("loop", "outer"), None)),
        check_vma=False,
    )
```

```python
import functools

import jax
import jax.numpy as jnp
from jax import lax
from jax.experimental import pallas as pl
from jax.experimental.pallas import tpu as pltpu
from jax.sharding import PartitionSpec as P

SHARED = 4
Z = 4
CORES = 2
X = 4
HEAD_PARTS = 4
BLOCK = SHARED * Z
MESH = pl.DeviceIdType.MESH
NT = (((1,), (1,)), ((), ()))
TN = (((0,), (0,)), ((), ()))


def dot(a, b, dims=(((1,), (0,)), ((), ()))):
    return lax.dot_general(a, b, dims, preferred_element_type=jnp.float32)


def terms(margins):
    t = jnp.exp(-jnp.abs(margins))
    r = 1.0 / (1.0 + t)
    return jnp.maximum(margins, 0.0) + jnp.log1p(t), jnp.where(margins >= 0.0, r, t * r)


def upper_half(shape):
    return lax.broadcasted_iota(jnp.int32, shape, 0) < SHARED


def pack(rows):
    w = rows.shape[1] // 4
    c = [rows[:, q * w : (q + 1) * w] for q in range(4)]
    up = upper_half(c[0].shape)
    lo = jnp.where(up, c[0], pltpu.roll(c[1], SHARED, 0))
    hi = jnp.where(up, c[2], pltpu.roll(c[3], SHARED, 0))
    return jnp.concatenate([lo, hi], axis=0)


def unpack_pair(first, second):
    up = upper_half((8, first.shape[1]))
    out = []
    for half in range(2):
        a, b = first[half * 8 : half * 8 + 8], second[half * 8 : half * 8 + 8]
        out.append(jnp.where(up, a, pltpu.roll(b, SHARED, 0)))
        out.append(jnp.where(up, pltpu.roll(a, SHARED, 0), b))
    return jnp.concatenate(out, axis=1)


def kernel(
    n_loop, ring,
    nf_hbm, ef_hbm, nh_hbm, eh_hbm, scale_hbm, table_hbm, index_hbm,
    loss_ref, ng, eg,
    nf, ef, nh, eh, scale_ref, table_ref, index_ref, nu, ru, ninv, rinv, ne, re, off, off_out,
    pieces_a, pieces_b, own_piece, W, G, S, R, held_a, own_a, sent_a, came_a, back_out, back, back_sum,
    slopes, local_slopes,
    lossacc, loss_out, loss_in, rup, rup_out, rup_in, nup, pre,
    load_sem, piece_send, recv_a, recv_b, ag_send, ag_recv, rs_send, rs_recv,
    fwd_send, fwd_recv, sum_send, sum_recv,
    back_send, back_recv, sib_send, sib_recv,
):
    pairs, width = nf.shape
    tile = min(256, width)
    tiles = width // tile
    l, o = lax.axis_index("loop"), lax.axis_index("outer")
    c, z, y = lax.rem(o, CORES), lax.rem(o // CORES, Z), o // (CORES * Z)
    x = lax.rem(l, X)
    y_first = lax.rem((x + 1) // 2, 2)
    z_first = y_first == 0
    side_a = x // 2
    side_b = 1 - side_a
    pod_a = lax.rem(l + n_loop - 1 + 2 * side_a, n_loop)
    pod_b = lax.rem(l + n_loop + 1 - 2 * side_a, n_loop)

    def outer(yy, zz, cc):
        return (yy * Z + zz) * CORES + cc

    below, above = lax.rem(l + n_loop - 1, n_loop), lax.rem(l + 1, n_loop)
    ys = [lax.rem(y + d, ring) for d in range(ring)]
    zs = [lax.rem(z + d, Z) for d in range(Z)]
    ys_back = [lax.rem(y + ring - d, ring) for d in range(ring)]
    zs_back = [lax.rem(z + Z - d, Z) for d in range(Z)]
    sibling = (l, outer(y, z, 1 - c))

    barrier = pltpu.get_barrier_semaphore()
    partners = [(pod_a, outer(y, zz, c)) for zz in zs] + [(pod_b, outer(yy, z, c)) for yy in ys]
    partners += [(l, outer(yy, z, c)) for yy in ys[1:]] + [(l, outer(y, zz, c)) for zz in zs[1:]] + [sibling]
    also = {True: [(pod_b, outer(y, zz, c)) for zz in zs[1:]], False: [(pod_a, outer(yy, z, c)) for yy in ys[1:]]}

    def greet(devices):
        for device in devices:
            pl.semaphore_signal(barrier, inc=1, device_id=device, device_id_type=MESH)

    greet(partners)

    @pl.when(z_first)
    def _():
        greet(also[True])

    @pl.when(jnp.logical_not(z_first))
    def _():
        greet(also[False])

    top_rows, deep = pl.ds(0, 16), nh.shape[0] // HEAD_PARTS
    other_rows = pl.ds(16, pairs - 16)
    moves = [(nf_hbm.at[top_rows], nf.at[top_rows])]
    for j in range(HEAD_PARTS):
        part = pl.ds(j * deep, deep)
        moves.append((nh_hbm.at[part], nh.at[part]))
    moves += [
        (nf_hbm.at[other_rows], nf.at[other_rows]), (eh_hbm, eh), (ef_hbm, ef),
        (scale_hbm, scale_ref), (table_hbm, table_ref), (index_hbm, index_ref),
    ]
    loads = [pltpu.make_async_copy(src, dst, load_sem.at[i]) for i, (src, dst) in enumerate(moves)]
    for load in loads:
        load.start()

    def remote(src, dst, send, recv, device):
        return pltpu.make_async_remote_copy(
            src_ref=src, dst_ref=dst, send_sem=send, recv_sem=recv, device_id=device, device_id_type=MESH
        )

    def project(feats, head, unit):
        def step(j, carry):
            cols = pl.ds(pl.multiple_of(j * tile, tile), tile)
            unit[:, cols] = dot(feats[...], head[:, cols])
            return carry

        lax.fori_loop(0, tiles, step, 0)

    def normalise(unit, inverse, emb):
        step_rows = min(64, pairs)

        def step(j, carry):
            rows = pl.ds(pl.multiple_of(j * step_rows, step_rows), step_rows)
            p = unit[rows, :]
            inv = lax.rsqrt(jnp.sum(p * p, axis=-1, keepdims=True) + 1e-06)
            u = p * inv
            inverse[rows, :] = inv
            unit[rows, :] = u
            emb[rows, :] = u.astype(jnp.bfloat16)
            return carry

        lax.fori_loop(0, pairs // step_rows, step, 0)

    loads[0].wait()
    top = None
    for j in range(HEAD_PARTS):
        loads[1 + j].wait()
        part = dot(nf[0:16, j * deep : (j + 1) * deep], nh[j * deep : (j + 1) * deep, :])
        top = part if top is None else top + part
    top = top[0:8, :]
    top = top * lax.rsqrt(jnp.sum(top * top, axis=-1, keepdims=True) + 1e-06)
    own_piece[...] = pack(top).astype(jnp.bfloat16)
    pl.semaphore_wait(barrier, len(partners) + len(also[True]) + (len(also[False]) - len(also[True])) * y_first)

    def piece_sends(along_z):
        copies = []
        for side, pod in enumerate((above, below)):
            for d in range(Z if along_z else ring):
                device = (pod, outer(y, zs[d], c) if along_z else outer(ys[d], z, c))
                landing, recv = (pieces_a, recv_a) if along_z else (pieces_b, recv_b)
                copies.append(
                    remote(own_piece, landing.at[d], piece_send.at[side * ring + d], recv.at[d], device)
                )
        return copies

    @pl.when(z_first)
    def _():
        for copy in piece_sends(True):
            copy.start()

    @pl.when(jnp.logical_not(z_first))
    def _():
        for copy in piece_sends(False):
            copy.start()

    loads[1 + HEAD_PARTS].wait()
    project(nf, nh, nu)
    normalise(nu, ninv, ne)

    for load in loads[2 + HEAD_PARTS :]:
        load.wait()
    project(ef, eh, ru)
    normalise(ru, rinv, re.at[pl.ds(0, pairs)])
    index = index_ref[...]
    offsets = jnp.zeros(index.shape, jnp.float32)
    for k in range(table_ref.shape[0]):
        offsets = jnp.where(index == k, table_ref[k], offsets)
    off_out[...] = jnp.broadcast_to(offsets, off_out.shape)
    sib_rec = remote(re.at[pl.ds(0, pairs)], re.at[pl.ds(pairs, pairs)], sib_send.at[0], sib_recv.at[0], sibling)
    sib_off = remote(off_out, off, sib_send.at[1], sib_recv.at[1], sibling)
    sib_rec.start()
    sib_off.start()
    scale = scale_ref[0]

    size = SHARED * ring
    far_first = sorted(range(1, ring), key=lambda d: -min(d, ring - d))

    def rows_b(d):
        return pl.ds(size * (Z + d), size)

    def forward(p, d):
        i = p * ring + d
        return remote(pieces_a.at[p], held_a.at[i], fwd_send.at[i], fwd_recv.at[i], (l, outer(ys[d], z, c)))

    def sum_a(p, d):
        i = p * ring + d
        return remote(sent_a.at[i], came_a.at[i], sum_send.at[i], sum_recv.at[i], (l, outer(ys_back[d], z, c)))

    forwards = {(p, d): forward(p, d) for p in range(Z) for d in far_first}
    sums_a = {(p, d): sum_a(p, d) for p in range(Z) for d in far_first}
    gathers, reduces = {}, {}
    for d in range(1, Z):
        gathers[d] = remote(
            W.at[rows_b(0)], W.at[rows_b(d)], ag_send.at[d], ag_recv.at[d], (l, outer(y, zs[d], c))
        )
        reduces[d] = remote(
            S.at[pl.ds(size * d, size)], R.at[pl.ds(size * d, size)], rs_send.at[d], rs_recv.at[d],
            (l, outer(y, zs_back[d], c)),
        )

    def unpacked(packed):
        return jnp.concatenate([unpack_pair(packed[d], packed[d + 1]) for d in range(0, len(packed), 2)], axis=0)

    for p in range(Z):
        remote(own_piece, pieces_a.at[p], piece_send.at[0], recv_a.at[p], sibling).wait_recv()
        for d in far_first:
            forwards[p, d].start()
    for d in range(ring):
        remote(own_piece, pieces_b.at[d], piece_send.at[0], recv_b.at[d], sibling).wait_recv()
    W[rows_b(0), :] = unpacked([pieces_b[d].astype(jnp.float32) for d in range(ring)]).astype(jnp.bfloat16)
    for d in (2, 1, 3):
        gathers[d].start()

    sims = dot(ne[...], re[0:pairs, :], NT)
    logits = scale * sims + offsets
    positive = lax.broadcasted_iota(jnp.int32, logits.shape, 0) == lax.broadcasted_iota(jnp.int32, logits.shape, 1)
    softplus, sigmoid = terms(jnp.where(positive, -logits, logits))
    local_slopes[...] = jnp.where(positive, -sigmoid, sigmoid).astype(jnp.bfloat16)
    lossacc[:, 0:pairs] = jnp.sum(softplus.reshape(pairs // 8, 8, pairs), axis=0)
    lossacc[:, pairs:] = jnp.zeros((8, pairs), jnp.float32)

    def back_grad(head, out):
        def step(j, carry):
            cols = pl.ds(pl.multiple_of(j * tile, tile), tile)
            out[:, cols] = dot(pre[...], head[cols, :], NT)
            return carry

        lax.fori_loop(0, tiles, step, 0)

    def pre_grads(unit, inverse, upstream):
        step_rows = min(64, pairs)

        def step(j, carry):
            rows = pl.ds(pl.multiple_of(j * step_rows, step_rows), step_rows)
            u, up = unit[rows, :], upstream(rows)
            radial = jnp.sum(u * up, axis=-1, keepdims=True)
            pre[rows, :] = (inverse[rows, :] * (up - u * radial)).astype(jnp.bfloat16)
            return carry

        lax.fori_loop(0, pairs // step_rows, step, 0)

    sib_off.wait_recv()
    sib_rec.wait_recv()
    all_offsets = jnp.concatenate([off_out[0:1, :], off[0:1, :]], axis=1)

    def work(start):
        rows = slice(start, start + size)
        logits = scale * dot(W[rows, :], re[...], NT) + all_offsets
        softplus, sigmoid = terms(logits)
        lossacc[...] += jnp.sum(softplus.reshape(size // 8, 8, 2 * pairs), axis=0)
        s = sigmoid.astype(jnp.bfloat16)
        slopes[rows, :] = s
        return dot(s, re[...])

    def work_b(d):
        gathers[d].wait_recv()
        S[pl.ds(size * d, size), :] = work(size * (Z + d)).astype(jnp.bfloat16)
        reduces[d].start()

    def work_a(p):
        for d in far_first:
            forwards[p, d].wait_recv()
        packed = [pieces_a[p]] + [held_a[p * ring + d] for d in range(1, ring)]
        W[size * p : size * (p + 1), :] = unpacked([q.astype(jnp.float32) for q in packed]).astype(jnp.bfloat16)
        grads = work(size * p)
        for d in [0] + far_first:
            half = grads[(d // 2) * 8 : (d // 2) * 8 + 8, :]
            if d % 2:
                half = pltpu.roll(half, SHARED, 0)
            if d == 0:
                own_a[p] = pack(half)
            else:
                sent_a[p * ring + d] = pack(half).astype(jnp.bfloat16)
                sums_a[p, d].start()

    G[...] = work(size * Z)

    def upstream_notes(j, carry):
        cols = pl.ds(pl.multiple_of(j * tile, tile), tile)
        nup[:, cols] = scale * dot(local_slopes[...], re[0:pairs, cols])
        return carry

    lax.fori_loop(0, tiles, upstream_notes, 0)
    pre_grads(nu, ninv, lambda rows: nup[rows, :])
    back_grad(nh, ng)
    work_a(0)
    work_b(1)
    work_a(1)
    work_b(3)
    work_a(2)
    work_b(2)
    work_a(3)

    def upstream_sibling(j, carry):
        cols = pl.ds(pl.multiple_of(j * tile, tile), tile)
        rup_out[:, cols] = dot(slopes[:, pairs:], W[:, cols], TN)
        return carry

    def upstream_own(j, carry):
        cols = pl.ds(pl.multiple_of(j * tile, tile), tile)
        rup[:, cols] = dot(slopes[:, 0:pairs], W[:, cols], TN) + dot(local_slopes[...], ne[:, cols], TN)
        return carry

    lax.fori_loop(0, tiles, upstream_sibling, 0)
    loss_out[...] = lossacc[:, pairs:]
    sib_rup = remote(rup_out, rup_in, sib_send.at[2], sib_recv.at[2], sibling)
    sib_loss = remote(loss_out, loss_in, sib_send.at[3], sib_recv.at[3], sibling)
    sib_rup.start()
    sib_loss.start()
    lax.fori_loop(0, tiles, upstream_own, 0)

    returns = []

    def give(i, d, kind):
        owner = outer(ys_back[d], z, c) if kind == "b" else outer(y, zs_back[d], c)
        pod, side = (pod_b, side_b) if kind == "b" else (pod_a, side_a)
        k = side * ring + d
        copy = remote(back_out.at[i], back.at[k], back_send.at[i], back_recv.at[k], (pod, owner))
        copy.start()
        returns.append(copy)

    def return_a(p):
        total = own_a[p]
        for d in far_first:
            sums_a[p, d].wait_recv()
            total = total + came_a[p * ring + d].astype(jnp.float32)
        back_out[p] = (scale * total).astype(jnp.bfloat16)
        give(p, p, "a")

    def return_b():
        total = G[...]
        for d in range(1, Z):
            reduces[d].wait_recv()
            total = total + R[pl.ds(size * d, size), :].astype(jnp.float32)
        total = scale * total
        for d in range(ring):
            half = total[(d // 2) * 8 : (d // 2) * 8 + 8, :]
            if d % 2:
                half = pltpu.roll(half, SHARED, 0)
            back_out[Z + d] = pack(half).astype(jnp.bfloat16)
            give(Z + d, d, "b")

    return_a(0)
    return_a(1)
    return_b()
    return_a(2)
    return_a(3)

    sib_rup.wait_recv()
    sib_loss.wait_recv()
    loss = jnp.sum(lossacc[:, 0:pairs] + loss_in[...], axis=0, keepdims=True)
    loss_ref[...] = loss * (1.0 / (pairs + ring * Z * CORES * SHARED * 2))
    pre_grads(ru, rinv, lambda rows: scale * (rup[rows, :] + rup_in[rows, :]))
    back_grad(eh, eg)

    def take_back(count):
        total = None
        for side in range(2):
            for d in range(count):
                k = side * ring + d
                remote(own_piece, back.at[k], back_send.at[0], back_recv.at[k], sibling).wait_recv()
                part = back[k].astype(jnp.float32)
                total = part if total is None else total + part
        back_sum[...] = total

    @pl.when(z_first)
    def _():
        take_back(Z)

    @pl.when(jnp.logical_not(z_first))
    def _():
        take_back(ring)

    lo, hi = back_sum[0:8, :], back_sum[8:16, :]
    spread = jnp.concatenate([lo, pltpu.roll(lo, SHARED, 0), hi, pltpu.roll(hi, SHARED, 0)], axis=1)
    up = nup[0:8, :] + jnp.where(upper_half(spread.shape), spread, 0.0)
    u = nu[0:8, :]
    radial = jnp.sum(u * up, axis=-1, keepdims=True)
    g = (ninv[0:8, :] * (up - u * radial)).astype(jnp.bfloat16)
    ng[0:8, :] = dot(g, nh[...], NT)

    @pl.when(z_first)
    def _():
        for copy in piece_sends(True):
            copy.wait_send()

    @pl.when(jnp.logical_not(z_first))
    def _():
        for copy in piece_sends(False):
            copy.wait_send()

    rings = list(forwards.values()) + list(sums_a.values())
    for copy in rings + list(gathers.values()) + list(reduces.values()) + returns:
        copy.wait_send()
    for copy in (sib_rec, sib_off, sib_rup, sib_loss):
        copy.wait_send()


def write_out(loss, ng, eg, loss_out, ng_out, eg_out, sem):
    copies = [
        pltpu.make_async_copy(src, dst, sem.at[i])
        for i, (src, dst) in enumerate(((ng, ng_out), (eg, eg_out), (loss, loss_out)))
    ]
    for copy in copies:
        copy.start()
    for copy in copies:
        copy.wait()


def in_hbm(a):
    return pltpu.with_memory_space_constraint(a, pltpu.HBM)


def per_device(n_loop, n_outer, note_feats, ehr_feats, note_head, ehr_head, logit_scale, bias_table, bias_index):
    pairs, width = note_feats.shape
    emb = note_head.shape[1]
    ring = n_outer // (Z * CORES)
    held = 2 * ring * BLOCK
    own = SHARED * ring
    bf16, f32 = jnp.bfloat16, jnp.float32
    vmem = pltpu.VMEM
    dma = pltpu.SemaphoreType.DMA
    hbm = pl.BlockSpec(memory_space=pltpu.HBM)
    whole = pl.BlockSpec(memory_space=pltpu.VMEM)
    outs = (
        jax.ShapeDtypeStruct((1, pairs), f32),
        jax.ShapeDtypeStruct((pairs, width), f32),
        jax.ShapeDtypeStruct((pairs, width), f32),
    )
    piece = (BLOCK, emb // 4)
    results = pl.pallas_call(
        functools.partial(kernel, n_loop, ring),
        out_shape=tuple(vmem(out.shape, f32) for out in outs),
        in_specs=[hbm] * 7,
        out_specs=(whole,) * 3,
        scratch_shapes=[
            vmem((pairs, width), bf16),
            vmem((pairs, width), bf16),
            vmem((width, emb), bf16),
            vmem((width, emb), bf16),
            pltpu.SMEM(logit_scale.shape, f32),
            pltpu.SMEM(bias_table.shape, f32),
            vmem((1, pairs), jnp.int32),
            vmem((pairs, emb), f32),
            vmem((pairs, emb), f32),
            vmem((pairs, 1), f32),
            vmem((pairs, 1), f32),
            vmem((pairs, emb), bf16),
            vmem((2 * pairs, emb), bf16),
            vmem((8, pairs), f32),
            vmem((8, pairs), f32),
            vmem((Z,) + piece, bf16),
            vmem((ring,) + piece, bf16),
            vmem(piece, bf16),
            vmem((held, emb), bf16),
            vmem((own, emb), f32),
            vmem((held // 2, emb), bf16),
            vmem((held // 2, emb), bf16),
            vmem((Z * ring,) + piece, bf16),
            vmem((Z,) + piece, f32),
            vmem((Z * ring,) + piece, bf16),
            vmem((Z * ring,) + piece, bf16),
            vmem((Z + ring,) + piece, bf16),
            vmem((2 * ring,) + piece, bf16),
            vmem(piece, f32),
            vmem((held, 2 * pairs), bf16),
            vmem((pairs, pairs), bf16),
            vmem((8, 2 * pairs), f32),
            vmem((8, pairs), f32),
            vmem((8, pairs), f32),
            vmem((pairs, emb), f32),
            vmem((pairs, emb), f32),
            vmem((pairs, emb), f32),
            vmem((pairs, emb), f32),
            vmem((pairs, emb), bf16),
            dma((7 + HEAD_PARTS,)),
            dma((2 * ring,)),
            dma((Z,)),
            dma((ring,)),
            dma((Z,)),
            dma((Z,)),
            dma((Z,)),
            dma((Z,)),
            dma((Z * ring,)),
            dma((Z * ring,)),
            dma((Z * ring,)),
            dma((Z * ring,)),
            dma((Z + ring,)),
            dma((2 * ring,)),
            dma((4,)),
            dma((4,)),
        ],
        compiler_params=pltpu.CompilerParams(
            collective_id=0, has_side_effects=True, vmem_limit_bytes=48 * 1024 * 1024
        ),
    )(
        in_hbm(note_feats), in_hbm(ehr_feats), in_hbm(note_head), in_hbm(ehr_head), logit_scale, in_hbm(bias_table),
        in_hbm(bias_index.reshape(1, pairs)),
    )
    loss, note_grad, ehr_grad = pl.pallas_call(
        write_out,
        out_shape=outs,
        in_specs=[whole] * 3,
        out_specs=(hbm,) * 3,
        scratch_shapes=[dma((3,))],
        compiler_params=pltpu.CompilerParams(vmem_limit_bytes=4 * 1024 * 1024),
    )(*results)
    return loss.reshape(pairs), note_grad, ehr_grad


def solution(mesh):
    return jax.shard_map(
        functools.partial(per_device, mesh.shape["loop"], mesh.shape["outer"]),
        mesh=mesh,
        in_specs=(
            P(("loop", "outer"), None),
            P(("loop", "outer"), None),
            P(),
            P(),
            P(),
            P(),
            P(("loop", "outer")),
        ),
        out_specs=(P(("loop", "outer")), P(("loop", "outer"), None), P(("loop", "outer"), None)),
        check_vma=False,
    )
```
